32 devices in a mesh: wide: 16 (over z, y, x), narrow: 2 (over core).
Axes of the slice: x: 2, y: 2, z: 4, core: 2. Of those that a mesh axis runs over, the one named last changes fastest.
Arguments:
- front: float32 [32768, 4096], P('wide', 'narrow'), as said below
- child_update: float32 [65536, 4096], P('wide', 'narrow'), may hold values from -0.8 to 0.8
- child_map: int32 [512], replicated, may hold values from -1 to 255, as said below
Outputs:
- factor: float32 [32768, 4096], P('wide', 'narrow')
The draws below stay inside these ranges and needn't reach their ends.
Inputs may be any that keep to these rules, and one draw needn't show every extreme that they name: `child_map`: entry m names the global row block of the front into which child block m is added, or -1 for an empty block. With F = 16, blocks m from p * 2F to p * 2F + 2F - 1 lie on wide index p; those with p < 8 belong to the first child, the others to the second. The first F of them name blocks whose index mod 16 is p mod (8), the last F blocks whose index mod 16 is p mod (8) + 8; within each group of F the named blocks increase and the empty entries come last. Each child names 192 distinct blocks, and one front owner receives a full group from each child. `front`: entries lie within -0.8 and 0.8, except on the global diagonal of the first 512 global columns, where a value between 5 and 40 times the square root of 512 is added.
All inputs are finite; a program needn't handle non-finite values.
Results may differ from the reference program's by a relative error of at most 0.0001.
Values sent between devices are 32-bit elements; how exact they have to be, the bound alone decides.
No kernel may reach another device: no remote copies, remote signals or barrier semaphores. Data moves between devices by JAX's collectives and lax.ppermute only.
A program may use at most 192 MiB of HBM per device.

```python
import math
import jax
import jax.numpy as jnp
from jax import lax

BS = 128
PW = 512
FRONT = 32768
WIN = 4096
CHILD = 24576
PANELS = 1
N_WIDE = 16
N_NARROW = 2


def draw_front(key, part):
    rows = jnp.arange(FRONT, dtype=jnp.int32)
    cols = jnp.arange(WIN, dtype=jnp.int32)
    per_owner = FRONT // BS // N_WIDE
    col_slots = WIN // PW // N_NARROW
    wide_of = rows // (per_owner * BS)
    global_row = (rows // BS % per_owner * N_WIDE + wide_of) * BS + rows % BS
    narrow_of = cols // (col_slots * PW)
    global_col = (cols // PW % col_slots * N_NARROW + narrow_of) * PW + cols % PW
    base = jax.random.uniform(jax.random.fold_in(key, 3), (FRONT, WIN), jnp.float32, -0.8, 0.8)
    leading = PANELS * PW
    widths = math.sqrt(leading)
    shifts = jnp.exp(jax.random.uniform(jax.random.fold_in(key, 5), (WIN,), jnp.float32, math.log(5.0), math.log(40.0))) * widths
    on_diagonal = (global_row[:, None] == global_col[None, :]) & (global_col[None, :] < leading)
    return base + jnp.where(on_diagonal, shifts[global_col][None, :], 0.0)


def draw_child_map(key, part):
    blocks = FRONT // BS
    per_owner = blocks // N_WIDE
    half_count = N_WIDE // 2
    slots_device = 2 * per_owner
    used = CHILD // BS
    ids = jnp.arange(blocks, dtype=jnp.int32)
    owners = ids % N_WIDE
    full_owner = jax.random.randint(jax.random.fold_in(key, 2), (), 0, N_WIDE)
    result = jnp.full((2 * blocks,), -1, jnp.int32)
    for child_index in range(2):
        subkey = jax.random.fold_in(key, 17 + child_index)
        shuffled = jax.random.permutation(jax.random.fold_in(subkey, 1), blocks).astype(jnp.int32)
        ranking = jnp.zeros((blocks,), jnp.int32).at[shuffled].set(ids)
        priority = jnp.where(owners == full_owner, ranking - blocks, ranking)
        picked_order = jnp.argsort(priority, stable=True)
        chosen = jnp.zeros((blocks,), jnp.int32).at[picked_order[:used]].set(1)
        grid = chosen.reshape(per_owner, N_WIDE)
        position = (jnp.cumsum(grid, axis=0) - grid).reshape(blocks)
        device = child_index * half_count + owners % half_count
        groups = owners // half_count
        destination = device * slots_device + groups * per_owner + position
        destination = jnp.where(chosen == 1, destination, 2 * blocks)
        result = result.at[destination].set(ids, mode='drop')
    return result


def shard_levels(own_key, shape, split, smallest, top_value):
    def one(dim, shards_of):
        heights = jax.random.uniform(jax.random.fold_in(jax.random.fold_in(own_key, 6), dim), (shards_of,), jnp.float32, smallest / len(split), top_value / len(split))
        return jnp.repeat(jnp.exp(heights), shape[dim] // shards_of).reshape((-1,) + (1,) * (len(shape) - dim - 1))

    gain = one(*split[0])
    for cut in split[1:]:
        gain = gain * one(*cut)
    return gain


def setup_inputs(seed: int = 0) -> dict:
    key_list = jax.random.split(jax.random.key(seed), 4)
    front = draw_front(jax.random.fold_in(key_list[3], 71), 0)
    child_update = jnp.clip(jax.random.uniform(key_list[1], (2 * FRONT, WIN), jnp.float32, -0.8, 0.8) * shard_levels(key_list[1], (2 * FRONT, WIN), ((0, 16), (1, 2)), -0.4, 0.0), -0.8, 0.8)
    child_map = draw_child_map(jax.random.fold_in(key_list[3], 71), 0)
    return {"front": front, "child_update": child_update, "child_map": child_map}


def global_order(stored):
    row_slots = FRONT // BS // N_WIDE
    col_slots = WIN // PW // N_NARROW
    shaped = stored.reshape(N_WIDE, row_slots, BS, N_NARROW, col_slots, PW)
    return shaped.transpose(1, 0, 2, 4, 3, 5).reshape(FRONT, WIN)

def stored_order(matrix):
    row_slots = FRONT // BS // N_WIDE
    col_slots = WIN // PW // N_NARROW
    shaped = matrix.reshape(row_slots, N_WIDE, BS, col_slots, N_NARROW, PW)
    return shaped.transpose(1, 0, 2, 4, 3, 5).reshape(FRONT, WIN)

def reference(front, child_update, child_map):
    block_count = FRONT // BS
    col_slots = WIN // PW // N_NARROW
    matrix = global_order(front)
    children = child_update.reshape(2 * block_count, BS, N_NARROW, col_slots, PW)
    children = children.transpose(0, 1, 3, 2, 4).reshape(2 * block_count, BS, WIN)
    col_blocks = jnp.arange(WIN // BS, dtype=jnp.int32)
    masks = []
    for child_index in range(2):
        names = child_map[child_index * block_count:(child_index + 1) * block_count]
        named = jnp.any(names[:, None] == col_blocks[None, :], axis=0)
        masks.append(jnp.repeat(named, BS))
    column_mask = jnp.stack(masks, 0)
    children = children.reshape(2, block_count, BS, WIN)
    children = jnp.where(column_mask[:, None, None, :], children, jnp.zeros_like(children))
    children = children.reshape(2 * block_count, BS, WIN)
    targets = jnp.where(child_map < 0, block_count, child_map).astype(jnp.int32)
    matrix = matrix.reshape(block_count, BS, WIN).at[targets].add(children, mode='drop').reshape(FRONT, WIN)
    for panel_index in range(PANELS):
        first_col = panel_index * PW
        next_col = first_col + PW
        diag_block = matrix[first_col:next_col, first_col:next_col]
        symmetric = jnp.tril(diag_block) + jnp.tril(diag_block, -1).T
        factor_diag = jnp.tril(jnp.linalg.cholesky(symmetric))
        below = lax.linalg.triangular_solve(factor_diag, matrix[next_col:, first_col:next_col], left_side=False, lower=True, transpose_a=True)
        panel = jnp.concatenate([jnp.zeros((first_col, PW), jnp.float32), factor_diag, below], 0)
        matrix = matrix.at[:, first_col:next_col].set(panel)
        update = jnp.dot(panel[next_col:].astype(jnp.float32), panel[next_col:WIN].T.astype(jnp.float32), precision=lax.Precision.HIGHEST, preferred_element_type=jnp.float32)
        matrix = matrix.at[next_col:, next_col:].add(-update)
    on_or_below = jnp.arange(FRONT)[:, None] >= jnp.arange(WIN)[None, :]
    matrix = jnp.where(on_or_below, matrix, jnp.zeros_like(matrix))
    return stored_order(matrix)
```

```python
import functools

import jax
import jax.numpy as jnp
from jax import lax
from jax.experimental import pallas as pl
from jax.experimental.pallas import tpu as pltpu
from jax.sharding import PartitionSpec as P

BS = 128
PW = 512
HALF = BS // 2
PIECES = PW // BS
FIRST = 40
HEAD = 88
SOON = 112
NEXT = 136
MIDDLE = 168
FIXED = 192
LATE = 96
MOVE = 64
CHUNK = 24
QUAD = 4
STRIP = 8
STRIPS = 4
RING = 8
ROW_GROUP = 4
VMEM_BYTES = 56 * 1024 * 1024
SMALL_COST = pl.CostEstimate(flops=1024, bytes_accessed=1024, transcendentals=0)

HIGHEST_PRECISION = lax.Precision.HIGHEST


def cross(value, half_count):
    size = lax.axis_size("wide")
    return lax.ppermute(value, "wide", [(i, i ^ half_count) for i in range(size)])


def core_swap(value):
    size = lax.axis_size("narrow")
    return lax.ppermute(value, "narrow", [(i, i ^ 1) for i in range(size)])


def from_first(value):
    size = lax.axis_size("narrow")
    if size == 2:
        moved = lax.ppermute(value, "narrow", [(0, 1)])
        return jnp.where(lax.axis_index("narrow") == 0, value, moved)
    mine = jnp.where(lax.axis_index("narrow") == 0, value, jnp.zeros_like(value))
    return lax.psum(mine, "narrow")


def far_pieces(piece):
    wide_count = lax.axis_size("wide")
    half_cols = piece.shape[1] // 2
    mine = lax.dynamic_slice_in_dim(piece, lax.axis_index("narrow") % 2 * half_cols, half_cols, 1)
    return [mine] + [cross(mine, mask) for mask in range(QUAD, wide_count, QUAD)]


def near_pieces(pieces):
    wide_index = lax.axis_index("wide")
    far = jnp.stack(pieces)
    quads, rows, half_cols = far.shape
    each = jnp.stack([far] + [cross(far, mask) for mask in range(1, QUAD)])
    bits = (QUAD * quads).bit_length() - 1
    each = each.reshape((2,) * bits + (rows, half_cols))
    masks = [QUAD >> shift for shift in range(1, QUAD.bit_length())]
    masks += [(QUAD * quads) >> shift for shift in range(1, quads.bit_length())]
    for axis, mask in enumerate(masks):
        each = jnp.where(wide_index // mask % 2 == 1, jnp.flip(each, axis), each)
    each = each.reshape(QUAD, quads, rows // BS, BS, half_cols)
    return each.transpose(2, 1, 0, 3, 4)


def tile_tables(child_map, source, front_slots, col_tiles):
    wide_count = lax.axis_size("wide")
    narrow_count = lax.axis_size("narrow")
    block_total = front_slots * wide_count
    side = source // (wide_count // 2)
    rows = lax.dynamic_slice_in_dim(child_map, (source * 2 + 1 - side) * front_slots, front_slots)
    names = lax.dynamic_slice_in_dim(child_map, side * block_total, block_total)
    tiles = jnp.arange(col_tiles, dtype=jnp.int32)
    first_core = lax.axis_index("narrow") // 2 * 2
    cores = first_core + jnp.arange(2, dtype=jnp.int32)
    global_tile = (tiles[None] // PIECES * narrow_count + cores[:, None]) * PIECES + tiles[None] % PIECES
    named = jnp.any(names[None, None, :] == global_tile[:, :, None], axis=2)
    need = named[:, :, None] & (rows[None, None, :] >= global_tile[:, :, None])
    need = need.reshape(2, col_tiles * front_slots)
    return rows, need


def chip_counts(child_map, front_slots, col_tiles):
    wide_count = lax.axis_size("wide")
    narrow_count = lax.axis_size("narrow")
    sides = jnp.arange(wide_count, dtype=jnp.int32) // (wide_count // 2)
    rows = child_map.reshape(wide_count, 2, front_slots)
    rows = jnp.where((sides == 0)[:, None], rows[:, 1], rows[:, 0])
    names = child_map.reshape(2, front_slots * wide_count)
    tiles = jnp.arange(col_tiles * narrow_count, dtype=jnp.int32)
    named = jnp.any(names[:, None, :] == tiles[None, :, None], axis=2)
    named = jnp.where((sides == 0)[:, None], named[:1], named[1:])
    each = jnp.sum(named[:, None, :] & (rows[:, :, None] >= tiles[None, None, :]), axis=1).astype(jnp.int32)
    each = each.reshape(wide_count, col_tiles // PIECES, narrow_count // 2, 2 * PIECES)
    return jnp.sum(each, axis=(1, 3))


def ranks(need):
    order = jnp.arange(need.shape[0], dtype=jnp.int32)
    return jnp.sum((order[None, :] < order[:, None]) & need[None, :], axis=1).astype(jnp.int32)


def sending_list(need):
    order = jnp.arange(need.shape[0], dtype=jnp.int32)
    hit = (ranks(need)[None, :] == order[:, None]) & need[None, :]
    return jnp.sum(jnp.where(hit, order[None, :], 0), axis=1).astype(jnp.int32)


def flows(counts, top):
    give = jnp.maximum(counts - top[..., None], 0)
    take = jnp.clip(top[..., None] - counts, 0, LATE)
    give_from = jnp.cumsum(give, axis=-1) - give
    take_from = jnp.cumsum(take, axis=-1) - take
    begin = jnp.maximum(give_from[..., :, None], take_from[..., None, :])
    end = jnp.minimum((give_from + give)[..., :, None], (take_from + take)[..., None, :])
    moved = jnp.maximum(end - begin, 0)
    feasible = (jnp.sum(give, axis=-1) <= jnp.sum(take, axis=-1)) & (jnp.max(moved, axis=(-2, -1)) <= MOVE)
    giver_at = top[..., None, None] + begin - give_from[..., :, None]
    taker_at = (top[..., None] - take - take_from)[..., None, :] + begin
    return moved, giver_at, taker_at, feasible


def lowest_top(counts, total):
    tops = FIXED + 4 * jnp.arange((total - FIXED) // 4 + 1, dtype=jnp.int32)
    _, _, _, feasible = flows(counts[None], jnp.broadcast_to(tops[:, None], (tops.shape[0], counts.shape[0])))
    return jnp.min(jnp.where(feasible, tops[:, None], total), axis=0).astype(jnp.int32)


def pack_kernel(split, front_slots, info, place, child, *refs):
    group, half = info[0], info[1]
    col_tiles = place.shape[0] // front_slots
    strips, in_sem, out_sem = refs[-3:]
    targets = [(0, split, refs[0], refs[1])]
    if len(refs) == 7:
        targets.append((split, place.shape[0] * 2, refs[2], refs[3]))

    def strip_in(j):
        slot = j % STRIPS
        row = pl.multiple_of((group + j) * BS, BS)
        return pltpu.make_async_copy(child.at[pl.ds(row, BS)], strips.at[slot], in_sem.at[slot])

    def tile_out(j, c, spot, kept_half, sent_half):
        slot = j % STRIPS
        col = pl.multiple_of(c * BS, BS)
        own = pl.multiple_of(half * HALF, HALF)
        other = pl.multiple_of((1 - half) * HALF, HALF)
        return (
            pltpu.make_async_copy(
                strips.at[slot, pl.ds(own, HALF), pl.ds(col, BS)], kept_half.at[spot], out_sem.at[0, slot]
            ),
            pltpu.make_async_copy(
                strips.at[slot, pl.ds(other, HALF), pl.ds(col, BS)], sent_half.at[spot], out_sem.at[1, slot]
            ),
        )

    def each_tile(j, act):
        def one(c, carry):
            spot = place[c * front_slots + j]

            for low, high, kept_half, sent_half in targets:

                @pl.when((spot >= low) & (spot < high))
                def _():
                    for copy in tile_out(j, c, spot - low, kept_half, sent_half):
                        act(copy)

            return carry

        lax.fori_loop(0, col_tiles, one, 0)

    for j in range(min(STRIPS - 1, front_slots)):
        strip_in(j).start()
    for j in range(front_slots):
        strip_in(j).wait()
        each_tile(j, lambda copy: copy.start())
        if j >= 1:
            each_tile(j - 1, lambda copy: copy.wait())
        if j + STRIPS - 1 < front_slots:
            strip_in(j + STRIPS - 1).start()
    each_tile(front_slots - 1, lambda copy: copy.wait())


def pack(child, info, place, sizes, front_slots):
    shapes = tuple(jax.ShapeDtypeStruct((size, HALF, BS), jnp.float32) for size in sizes for _ in range(2))
    smem = pl.BlockSpec(memory_space=pltpu.SMEM)
    hbm = pl.BlockSpec(memory_space=pl.ANY)
    return pl.pallas_call(
        functools.partial(pack_kernel, sizes[0], front_slots),
        out_shape=shapes,
        in_specs=[smem, smem, hbm],
        out_specs=(hbm,) * len(shapes),
        scratch_shapes=[
            pltpu.VMEM((STRIPS, BS, child.shape[1]), jnp.float32),
            pltpu.SemaphoreType.DMA((STRIPS,)),
            pltpu.SemaphoreType.DMA((2, STRIPS)),
        ],
        compiler_params=pltpu.CompilerParams(vmem_limit_bytes=VMEM_BYTES),
        cost_estimate=SMALL_COST,
        name="pack_tiles",
    )(info, place, child)


def tile_add_kernel(front_slots, info, listed, rows, acc_in, own, other, acc, held, part, done, in_sem, out_sem):
    begin, end, place, half = info[0], info[1], info[2], info[3]
    wide_count, narrow_index, narrow_count = info[4], info[5], info[6]

    def spot(i):
        k = listed[i]
        col_tile = k // front_slots
        row_block = rows[k % front_slots]
        row = pl.multiple_of(row_block // wide_count * BS, BS)
        col = pl.multiple_of(col_tile * BS, BS)
        global_tile = (col_tile // PIECES * narrow_count + narrow_index) * PIECES + col_tile % PIECES
        return row, col, row_block == global_tile

    def copies_in(i):
        slot = i % RING
        row, col, _ = spot(i)
        at = place + i
        mine = pl.multiple_of(half * HALF, HALF)
        its = pl.multiple_of((1 - half) * HALF, HALF)
        return (
            pltpu.make_async_copy(acc.at[pl.ds(row, BS), pl.ds(col, BS)], held.at[slot], in_sem.at[0, slot]),
            pltpu.make_async_copy(own.at[at], part.at[slot, pl.ds(mine, HALF)], in_sem.at[1, slot]),
            pltpu.make_async_copy(other.at[at], part.at[slot, pl.ds(its, HALF)], in_sem.at[2, slot]),
        )

    def copy_out(i):
        slot = i % RING
        row, col, _ = spot(i)
        return pltpu.make_async_copy(done.at[slot], acc.at[pl.ds(row, BS), pl.ds(col, BS)], out_sem.at[slot])

    def issue(i):
        @pl.when(i < end)
        def _():
            for copy in copies_in(i):
                copy.start()

    for ahead in range(RING - 1):
        issue(begin + ahead)

    def step(i, carry):
        issue(i + RING - 1)
        for copy in copies_in(i):
            copy.wait()

        @pl.when(i - RING >= begin)
        def _():
            copy_out(i - RING).wait()

        slot = i % RING
        _, _, diagonal = spot(i)
        below = lax.broadcasted_iota(jnp.int32, (BS, BS), 0) >= lax.broadcasted_iota(jnp.int32, (BS, BS), 1)
        total = held[slot] + part[slot]
        done[slot] = jnp.where(below | jnp.logical_not(diagonal), total, 0.0)
        copy_out(i).start()
        return carry

    lax.fori_loop(begin, end, step, 0)

    def drain(i, carry):
        copy_out(i).wait()
        return carry

    lax.fori_loop(jnp.maximum(begin, end - RING), end, drain, 0)


def tile_add(acc, own, other, info, listed, rows, front_slots):
    smem = pl.BlockSpec(memory_space=pltpu.SMEM)
    hbm = pl.BlockSpec(memory_space=pl.ANY)
    return pl.pallas_call(
        functools.partial(tile_add_kernel, front_slots),
        out_shape=jax.ShapeDtypeStruct(acc.shape, acc.dtype),
        in_specs=[smem, smem, smem, hbm, hbm, hbm],
        out_specs=hbm,
        scratch_shapes=[
            pltpu.VMEM((RING, BS, BS), jnp.float32),
            pltpu.VMEM((RING, BS, BS), jnp.float32),
            pltpu.VMEM((RING, BS, BS), jnp.float32),
            pltpu.SemaphoreType.DMA((3, RING)),
            pltpu.SemaphoreType.DMA((RING,)),
        ],
        input_output_aliases={3: 0},
        cost_estimate=SMALL_COST,
        name="add_tiles",
    )(info, listed, rows, acc, own, other)


def panel_base_kernel(kept_row, present, front, kept, mask, out):
    s = pl.program_id(0)
    take = (mask[...] > 0) & (present[s] > 0)
    out[...] = front[...] + jnp.where(take, kept[...], 0.0)


def panel_base(front, child, kept_row, present, mask):
    local_rows = front.shape[0]
    return pl.pallas_call(
        panel_base_kernel,
        out_shape=jax.ShapeDtypeStruct((local_rows, PW), jnp.float32),
        grid_spec=pltpu.PrefetchScalarGridSpec(
            num_scalar_prefetch=2,
            grid=(local_rows // BS,),
            in_specs=[
                pl.BlockSpec((BS, PW), lambda s, kept_row, present: (s, 0)),
                pl.BlockSpec((BS, PW), lambda s, kept_row, present: (kept_row[s], 0)),
                pl.BlockSpec((1, PW), lambda s, kept_row, present: (0, 0)),
            ],
            out_specs=pl.BlockSpec((BS, PW), lambda s, kept_row, present: (s, 0)),
        ),
        cost_estimate=SMALL_COST,
        name="panel_base",
    )(kept_row, present, front, child, mask)


def exact_dot(left, right, contract):
    return lax.dot_general(
        left, right, (contract, ((), ())), precision=HIGHEST_PRECISION, preferred_element_type=jnp.float32
    )


def factor_kernel(diag, lower, inverse, work, pair):
    size = diag.shape[0]
    full = diag[...]
    row = lax.broadcasted_iota(jnp.int32, (size, size), 0)
    col = lax.broadcasted_iota(jnp.int32, (size, size), 1)
    work[...] = jnp.where(row >= col, full, full.T)
    lower[...] = jnp.zeros_like(lower)
    inverse[...] = jnp.zeros_like(inverse)
    block_row = lax.broadcasted_iota(jnp.int32, (BS, BS), 0)
    block_col = lax.broadcasted_iota(jnp.int32, (BS, BS), 1)
    strip_row = lax.broadcasted_iota(jnp.int32, (STRIP, 2 * BS), 0)
    strip_lane = lax.broadcasted_iota(jnp.int32, (STRIP, 2 * BS), 1)
    for k in range(size // BS):
        here = slice(k * BS, (k + 1) * BS)
        pair[:, :BS] = work[here, here]
        pair[:, BS:] = jnp.where(block_row == block_col, 1.0, 0.0)

        def eliminate(step, carry):
            top = pl.multiple_of(step * STRIP, STRIP)
            strip = pair[pl.ds(top, STRIP), :]
            for j in range(STRIP):
                column = jnp.sum(jnp.where(strip_lane == top + j, strip, 0.0), axis=1, keepdims=True)
                scale = lax.rsqrt(column[j : j + 1])
                pivot = strip[j : j + 1] * scale
                reduced = strip - (column * scale) * pivot
                strip = jnp.where(strip_row > j, reduced, jnp.where(strip_row == j, pivot, strip))
            pair[pl.ds(top, STRIP), :] = strip
            ahead = jnp.where(strip_lane[:, :BS] >= top + STRIP, strip[:, :BS], 0.0)
            pair[...] -= exact_dot(ahead.T, strip, ((1,), (0,)))
            return carry

        lax.fori_loop(0, BS // STRIP, eliminate, 0)
        own_inverse = jnp.where(block_row >= block_col, pair[:, BS:], 0.0)
        lower[here, here] = jnp.where(block_row <= block_col, pair[:, :BS], 0.0).T
        inverse[here, here] = own_inverse
        if (k + 1) * BS < size:
            below = slice((k + 1) * BS, size)
            column_block = exact_dot(work[below, here], own_inverse, ((1,), (1,)))
            lower[below, here] = column_block
            work[below, below] -= exact_dot(column_block, column_block, ((1,), (1,)))
        if k:
            before = slice(0, k * BS)
            product = exact_dot(lower[here, before], inverse[before, before], ((1,), (0,)))
            inverse[here, before] = -exact_dot(own_inverse, product, ((1,), (0,)))


def factor_block(diag):
    shape = jax.ShapeDtypeStruct(diag.shape, jnp.float32)
    return pl.pallas_call(
        factor_kernel,
        out_shape=(shape, shape),
        scratch_shapes=[pltpu.VMEM(diag.shape, jnp.float32), pltpu.VMEM((BS, 2 * BS), jnp.float32)],
        compiler_params=pltpu.CompilerParams(vmem_limit_bytes=VMEM_BYTES),
        cost_estimate=SMALL_COST,
        name="factor_block",
    )(diag)


def solve_kernel(with_diagonal, where, rows, inverse, lower, out):
    out[...] = exact_dot(rows[...], inverse[...], ((1,), (1,)))
    if with_diagonal:
        wide_index, wide_count = where[0], where[1]
        for part in range(rows.shape[0] // BS):
            row_block = (pl.program_id(0) * ROW_GROUP + part) * wide_count + wide_index

            @pl.when(row_block < PIECES)
            def _():
                start = pl.multiple_of(row_block * BS, BS)
                out[part * BS : (part + 1) * BS, :] = lower[pl.ds(start, BS), :]


def solve(rows, inverse, lower, where, with_diagonal):
    tall = ROW_GROUP * BS
    whole = pl.BlockSpec((PW, PW), lambda g, where: (0, 0))
    strip = pl.BlockSpec((tall, PW), lambda g, where: (g, 0))
    return pl.pallas_call(
        functools.partial(solve_kernel, with_diagonal),
        out_shape=jax.ShapeDtypeStruct(rows.shape, jnp.float32),
        grid_spec=pltpu.PrefetchScalarGridSpec(
            num_scalar_prefetch=1,
            grid=(rows.shape[0] // tall,),
            in_specs=[strip, whole, whole],
            out_specs=strip,
        ),
        compiler_params=pltpu.CompilerParams(vmem_limit_bytes=VMEM_BYTES),
        cost_estimate=SMALL_COST,
        name="solve_rows",
    )(where, rows, inverse, lower)


def update_kernel(kept_row, present, where, front, kept0, kept1, kept2, kept3, mask, factor, rhs, out, rhs_high, rhs_low):
    g = pl.program_id(0)

    @pl.when(g == 0)
    def _():
        rhs_high[...] = rhs[...].astype(jnp.bfloat16)
        rhs_low[...] = (rhs[...] - rhs_high[...].astype(jnp.float32)).astype(jnp.bfloat16)

    wide_index, wide_count, narrow_index, narrow_count = where[0], where[1], where[2], where[3]
    left = factor[...]
    left_high = left.astype(jnp.bfloat16)
    left_low = (left - left_high.astype(jnp.float32)).astype(jnp.bfloat16)
    rows = left.shape[0]
    col_slots = out.shape[1] // PW
    row_local = lax.broadcasted_iota(jnp.int32, (rows, PW), 0)
    slot = g * ROW_GROUP + row_local // BS
    global_row = (slot * wide_count + wide_index) * BS + row_local % BS
    col_in_block = lax.broadcasted_iota(jnp.int32, (rows, PW), 1)
    dims = (((1,), (1,)), ((), ()))
    for t in range(col_slots):
        cols = pl.ds(t * PW, PW)
        column_block = t * narrow_count + narrow_index
        high = rhs_high[cols, :]
        low = rhs_low[cols, :]
        product = lax.dot_general(left_high, high, dims, preferred_element_type=jnp.float32)
        product += lax.dot_general(left_high, low, dims, preferred_element_type=jnp.float32)
        product += lax.dot_general(left_low, high, dims, preferred_element_type=jnp.float32)
        below = global_row >= column_block * PW + col_in_block
        take = mask[:, cols] > 0
        for part, kept in enumerate((kept0, kept1, kept2, kept3)):
            rows_here = slice(part * BS, (part + 1) * BS)
            there = take & (present[g * ROW_GROUP + part] > 0)
            base = front[rows_here, cols] + jnp.where(there, kept[:, cols], 0.0)
            value = base - product[rows_here]
            if t == 0:
                value = jnp.where(column_block > 0, value, left[rows_here])
            out[rows_here, cols] = jnp.where(below[rows_here], value, 0.0)


def update(front, child, kept_row, present, where, mask, factor, rhs):
    local_rows, local_cols = front.shape
    tall = ROW_GROUP * BS

    def kept_spec(part):
        return pl.BlockSpec(
            (BS, local_cols), lambda g, kept_row, present, where: (kept_row[g * ROW_GROUP + part], 0)
        )

    def fixed(shape):
        return pl.BlockSpec(shape, lambda g, kept_row, present, where: (0, 0))

    def tall_spec(width):
        return pl.BlockSpec((tall, width), lambda g, kept_row, present, where: (g, 0))

    return pl.pallas_call(
        update_kernel,
        out_shape=jax.ShapeDtypeStruct(front.shape, jnp.float32),
        grid_spec=pltpu.PrefetchScalarGridSpec(
            num_scalar_prefetch=3,
            grid=(local_rows // tall,),
            in_specs=[tall_spec(local_cols)]
            + [kept_spec(part) for part in range(ROW_GROUP)]
            + [
                fixed((1, local_cols)),
                tall_spec(PW),
                fixed((local_cols, PW)),
            ],
            out_specs=tall_spec(local_cols),
            scratch_shapes=[
                pltpu.VMEM((local_cols, PW), jnp.bfloat16),
                pltpu.VMEM((local_cols, PW), jnp.bfloat16),
            ],
        ),
        compiler_params=pltpu.CompilerParams(vmem_limit_bytes=VMEM_BYTES),
        cost_estimate=SMALL_COST,
        name="trailing_update",
    )(kept_row, present, where, front, child, child, child, child, mask, factor, rhs)


def shards(front, child_update, child_map):
    wide_count = lax.axis_size("wide")
    narrow_count = lax.axis_size("narrow")
    wide_index = lax.axis_index("wide")
    narrow_index = lax.axis_index("narrow")
    half_count = wide_count // 2
    local_rows, local_cols = front.shape
    front_slots = local_rows // BS
    col_slots = local_cols // PW
    col_tiles = local_cols // BS
    block_total = front_slots * wide_count
    child_side = wide_index // half_count
    partner = wide_index ^ half_count
    core = narrow_index % 2
    total = 2 * front_slots * col_tiles

    _, send_need = tile_tables(child_map, wide_index, front_slots, col_tiles)
    got_rows, got_need = tile_tables(child_map, partner, front_slots, col_tiles)
    send_counts = jnp.sum(send_need, axis=1).astype(jnp.int32)
    got_counts = jnp.sum(got_need, axis=1).astype(jnp.int32)
    own_need = jnp.where(core == 0, send_need[0], send_need[1])
    got_list = sending_list(jnp.where(core == 0, got_need[0], got_need[1]))
    send_base = jnp.where(core == 0, 0, send_counts[0])
    send_place = jnp.where(own_need, send_base + ranks(own_need), -1).astype(jnp.int32)
    got_base = jnp.where(core == 0, 0, got_counts[0])
    got_count = jnp.where(core == 0, got_counts[0], got_counts[1])
    pack_info = jnp.stack([(1 - child_side) * front_slots, core]).astype(jnp.int32)

    head_split = min(HEAD, total)
    has_more = total > HEAD

    def joined(kept_half, swapped, low):
        at = low + jnp.arange(kept_half.shape[0], dtype=jnp.int32)
        is_own = (at >= send_counts[0]) == (core == 1)
        return jnp.where(is_own[:, None, None], kept_half, swapped)

    room = total - head_split + LATE
    packed = pack(
        child_update, pack_info, send_place, [head_split, room] if has_more else [head_split], front_slots
    )
    head = joined(packed[0], core_swap(packed[1]), 0)
    first_split = min(FIRST, head_split)
    heads = [(0, first_split, cross(head[:first_split], half_count))]
    second = head[first_split:]
    if has_more:
        counts = lax.dynamic_index_in_dim(
            chip_counts(child_map, front_slots, col_tiles), narrow_index // 2, 1, keepdims=False
        )
        counts = jnp.maximum(counts, FIXED).reshape(wide_count // QUAD, QUAD)
        tops = lowest_top(counts, total)
        moved, giver_at, taker_at, _ = flows(counts, tops)
        send_top = tops[wide_index // QUAD]
        got_top = tops[partner // QUAD]
        member = wide_index % QUAD
        send_quad = (moved[wide_index // QUAD], giver_at[wide_index // QUAD], taker_at[wide_index // QUAD])
        got_quad = (moved[partner // QUAD], giver_at[partner // QUAD], taker_at[partner // QUAD])

        rest = joined(packed[2], core_swap(packed[3]), head_split)
        soon = rest[: SOON - head_split]

        given = [
            lax.dynamic_slice_in_dim(rest, send_quad[1][member, member ^ mask] - head_split, MOVE)
            for mask in range(1, QUAD)
        ]
        second, soon, given, rest = lax.optimization_barrier((second, soon, given, rest))
        taken = [cross(given[mask - 1], mask) for mask in range(1, QUAD)]
    if first_split < head_split:
        heads.append((first_split, head_split, cross(second, half_count)))

    own_map = lax.dynamic_slice_in_dim(child_map, (wide_index * 2 + child_side) * front_slots, front_slots)
    target = wide_index + wide_count * jnp.arange(front_slots, dtype=jnp.int32)
    kept_hit = own_map[None, :] == target[:, None]
    present = jnp.any(kept_hit, axis=1).astype(jnp.int32)
    kept_slot = jnp.sum(jnp.where(kept_hit, jnp.arange(front_slots, dtype=jnp.int32)[None, :], 0), axis=1)
    kept_row = (child_side * front_slots + kept_slot).astype(jnp.int32)
    col_local = jnp.arange(local_cols, dtype=jnp.int32)
    global_col = (col_local // PW * narrow_count + narrow_index) * PW + col_local % PW
    names = lax.dynamic_slice_in_dim(child_map, child_side * block_total, block_total)
    named_cols = jnp.any(names[:, None] == (global_col // BS)[None, :], axis=0).astype(jnp.int32)[None, :]
    panel = panel_base(front, child_update, kept_row, present, named_cols[:, :PW])

    if has_more:
        got_soon = cross(soon, half_count)

    panel_count = jnp.where(
        narrow_index == 0, jnp.sum(got_need[0, : PIECES * front_slots]).astype(jnp.int32), 0
    )

    def add(matrix, tiles, first, last, low, high, other=None):
        begin = jnp.maximum(jnp.maximum(low - got_base, 0), first)
        end = jnp.minimum(jnp.minimum(high - got_base, got_count), last)
        info = jnp.stack(
            [
                begin,
                jnp.maximum(begin, end),
                got_base - low,
                core,
                jnp.int32(wide_count),
                narrow_index,
                jnp.int32(narrow_count),
            ]
        ).astype(jnp.int32)
        other = core_swap(tiles) if other is None else other
        return tile_add(matrix, tiles, other, info, got_list, got_rows, front_slots)

    heads = [(low, high, tiles, core_swap(tiles)) for low, high, tiles in heads]
    for low, high, tiles, other in heads:
        panel = add(panel, tiles, 0, panel_count, low, high, other)
    if has_more:
        panel, taken, got_soon = lax.optimization_barrier((panel, taken, got_soon))
        got_next = cross(rest[SOON - head_split : NEXT - head_split], half_count)
    panel = from_first(panel)

    window = local_cols * narrow_count
    window_slots = max(1, window // (BS * wide_count))
    pieces = far_pieces(panel[: window_slots * BS])
    if has_more:
        after = rest[MIDDLE - head_split : FIXED - head_split]
        body = rest[NEXT - head_split : MIDDLE - head_split]
        pieces, got_next, taken, body = lax.optimization_barrier((pieces, got_next, taken, body))
        got_body = cross(body, half_count)
        relayed = rest
        for mask in range(1, QUAD):
            at = send_quad[2][member ^ mask, member] - head_split
            kept_there = lax.dynamic_slice_in_dim(relayed, at, MOVE)
            valid = jnp.arange(MOVE, dtype=jnp.int32) < send_quad[0][member ^ mask, member]
            relayed = lax.dynamic_update_slice_in_dim(
                relayed, jnp.where(valid[:, None, None], taken[mask - 1], kept_there), at, 0
            )
        send_late = jnp.maximum(send_top - LATE, FIXED)
        got_late = jnp.maximum(got_top - LATE, FIXED)
        late = lax.dynamic_slice_in_dim(relayed, send_late - head_split, LATE)

    gathered = near_pieces(pieces)
    diag_half = gathered[0, 0].reshape(PW, PW // 2)
    by_rows = gathered.reshape(-1, PW // 2)[:window].reshape(col_slots, narrow_count, PW, PW // 2)

    def whole_rows(mine, others):
        return jnp.where(
            core == 0, jnp.concatenate([mine, others], 1), jnp.concatenate([others, mine], 1)
        )

    def rows_of(index):
        return lax.dynamic_index_in_dim(by_rows, index, 1, keepdims=False).reshape(local_cols, PW // 2)

    diag_block = whole_rows(diag_half, core_swap(diag_half))
    if has_more:
        diag_block, late, after, got_body = lax.optimization_barrier((diag_block, late, after, got_body))
        got_late_tiles = cross(late, half_count)
        got_after = cross(after, half_count)
    raw_rows = whole_rows(rows_of(narrow_index), core_swap(rows_of(narrow_index ^ 1)))
    factor_diag, inverse = factor_block(diag_block)

    where = jnp.stack(
        [wide_index, jnp.int32(wide_count), narrow_index, jnp.int32(narrow_count)]
    ).astype(jnp.int32)
    factor = solve(panel, inverse, factor_diag, where, True)
    panel_rows = solve(raw_rows, inverse, factor_diag, where, False)
    matrix = update(front, child_update, kept_row, present, where, named_cols, factor, panel_rows)

    for low, high, tiles, other in heads:
        matrix = add(matrix, tiles, panel_count, total, low, high, other)
    if has_more:
        matrix = add(matrix, got_soon, panel_count, total, head_split, SOON)
        matrix = add(matrix, got_next, panel_count, total, SOON, NEXT)
        matrix = add(matrix, got_body, panel_count, total, NEXT, MIDDLE)
        got_late_tiles, matrix = lax.optimization_barrier((got_late_tiles, matrix))
        returned = []
        for mask in range(1, QUAD):
            at = got_quad[2][member ^ mask, member] - got_late
            padded = jnp.concatenate([got_late_tiles, jnp.zeros_like(got_late_tiles[:MOVE])], 0)
            returned.append(cross(lax.dynamic_slice_in_dim(padded, at, MOVE), mask))
        matrix = add(matrix, got_late_tiles, panel_count, total, got_late, got_top)
        got_after, matrix = lax.optimization_barrier((got_after, matrix))
        steps = (jnp.max(tops) - LATE - FIXED + CHUNK - 1) // CHUNK

        def add_chunk(matrix, tiles, i):
            low = FIXED + (i - 1) * CHUNK
            high = jnp.where(i > 0, jnp.minimum(low + CHUNK, got_late), low)
            return add(matrix, tiles, panel_count, total, low, high)

        def tail(i, carried):
            matrix, tiles = carried
            low = FIXED + i * CHUNK
            got = cross(lax.dynamic_slice_in_dim(relayed, low - head_split, CHUNK), half_count)
            return add_chunk(matrix, tiles, i), got

        matrix, last = lax.fori_loop(0, steps, tail, (matrix, got_after[:CHUNK]))
        matrix = add_chunk(matrix, last, jnp.maximum(steps, 0))
        returned, matrix = lax.optimization_barrier((returned, matrix))
        matrix = add(matrix, got_after, panel_count, total, MIDDLE, FIXED)
        for mask in range(1, QUAD):
            low = got_quad[1][member, member ^ mask]
            high = low + got_quad[0][member, member ^ mask]
            matrix = add(matrix, returned[mask - 1], panel_count, total, low, high)
    return matrix


def solution(mesh):
    placed = (P("wide", "narrow"), P("wide", "narrow"), P())
    return jax.shard_map(
        shards, mesh=mesh, in_specs=placed, out_specs=P("wide", "narrow"), check_vma=False
    )
```

```python
import functools

import jax
import jax.numpy as jnp
from jax import lax
from jax.experimental import pallas as pl
from jax.experimental.pallas import tpu as pltpu
from jax.sharding import PartitionSpec as P

BS = 128
PW = 512
HALF = BS // 2
PIECES = PW // BS
FIRST = 40
HEAD = 88
SOON = 112
NEXT = 136
FIXED = 192
LATE = 96
MOVE = 64
CHUNK = 24
QUAD = 4
STRIP = 8
STRIPS = 4
RING = 8
ROW_GROUP = 4
VMEM_BYTES = 56 * 1024 * 1024
SMALL_COST = pl.CostEstimate(flops=1024, bytes_accessed=1024, transcendentals=0)

HIGHEST_PRECISION = lax.Precision.HIGHEST


def cross(value, half_count):
    size = lax.axis_size("wide")
    return lax.ppermute(value, "wide", [(i, i ^ half_count) for i in range(size)])


def core_swap(value):
    size = lax.axis_size("narrow")
    return lax.ppermute(value, "narrow", [(i, i ^ 1) for i in range(size)])


def from_first(value):
    size = lax.axis_size("narrow")
    if size == 2:
        moved = lax.ppermute(value, "narrow", [(0, 1)])
        return jnp.where(lax.axis_index("narrow") == 0, value, moved)
    mine = jnp.where(lax.axis_index("narrow") == 0, value, jnp.zeros_like(value))
    return lax.psum(mine, "narrow")


def far_pieces(piece):
    wide_count = lax.axis_size("wide")
    half_cols = piece.shape[1] // 2
    mine = lax.dynamic_slice_in_dim(piece, lax.axis_index("narrow") % 2 * half_cols, half_cols, 1)
    return [mine] + [cross(mine, mask) for mask in range(QUAD, wide_count, QUAD)]


def near_pieces(pieces):
    wide_index = lax.axis_index("wide")
    far = jnp.stack(pieces)
    quads, rows, half_cols = far.shape
    each = jnp.stack([far] + [cross(far, mask) for mask in range(1, QUAD)])
    bits = (QUAD * quads).bit_length() - 1
    each = each.reshape((2,) * bits + (rows, half_cols))
    masks = [QUAD >> shift for shift in range(1, QUAD.bit_length())]
    masks += [(QUAD * quads) >> shift for shift in range(1, quads.bit_length())]
    for axis, mask in enumerate(masks):
        each = jnp.where(wide_index // mask % 2 == 1, jnp.flip(each, axis), each)
    each = each.reshape(QUAD, quads, rows // BS, BS, half_cols)
    return each.transpose(2, 1, 0, 3, 4)


def tile_tables(child_map, source, front_slots, col_tiles):
    wide_count = lax.axis_size("wide")
    narrow_count = lax.axis_size("narrow")
    block_total = front_slots * wide_count
    side = source // (wide_count // 2)
    rows = lax.dynamic_slice_in_dim(child_map, (source * 2 + 1 - side) * front_slots, front_slots)
    names = lax.dynamic_slice_in_dim(child_map, side * block_total, block_total)
    tiles = jnp.arange(col_tiles, dtype=jnp.int32)
    first_core = lax.axis_index("narrow") // 2 * 2
    cores = first_core + jnp.arange(2, dtype=jnp.int32)
    global_tile = (tiles[None] // PIECES * narrow_count + cores[:, None]) * PIECES + tiles[None] % PIECES
    named = jnp.any(names[None, None, :] == global_tile[:, :, None], axis=2)
    need = named[:, :, None] & (rows[None, None, :] >= global_tile[:, :, None])
    need = need.reshape(2, col_tiles * front_slots)
    return rows, need


def chip_counts(child_map, front_slots, col_tiles):
    wide_count = lax.axis_size("wide")
    narrow_count = lax.axis_size("narrow")
    sides = jnp.arange(wide_count, dtype=jnp.int32) // (wide_count // 2)
    rows = child_map.reshape(wide_count, 2, front_slots)
    rows = jnp.where((sides == 0)[:, None], rows[:, 1], rows[:, 0])
    names = child_map.reshape(2, front_slots * wide_count)
    tiles = jnp.arange(col_tiles * narrow_count, dtype=jnp.int32)
    named = jnp.any(names[:, None, :] == tiles[None, :, None], axis=2)
    named = jnp.where((sides == 0)[:, None], named[:1], named[1:])
    each = jnp.sum(named[:, None, :] & (rows[:, :, None] >= tiles[None, None, :]), axis=1).astype(jnp.int32)
    each = each.reshape(wide_count, col_tiles // PIECES, narrow_count // 2, 2 * PIECES)
    return jnp.sum(each, axis=(1, 3))


def ranks(need):
    order = jnp.arange(need.shape[0], dtype=jnp.int32)
    return jnp.sum((order[None, :] < order[:, None]) & need[None, :], axis=1).astype(jnp.int32)


def sending_list(need):
    order = jnp.arange(need.shape[0], dtype=jnp.int32)
    hit = (ranks(need)[None, :] == order[:, None]) & need[None, :]
    return jnp.sum(jnp.where(hit, order[None, :], 0), axis=1).astype(jnp.int32)


def flows(counts, top):
    give = jnp.maximum(counts - top[..., None], 0)
    take = jnp.clip(top[..., None] - counts, 0, LATE)
    give_from = jnp.cumsum(give, axis=-1) - give
    take_from = jnp.cumsum(take, axis=-1) - take
    begin = jnp.maximum(give_from[..., :, None], take_from[..., None, :])
    end = jnp.minimum((give_from + give)[..., :, None], (take_from + take)[..., None, :])
    moved = jnp.maximum(end - begin, 0)
    feasible = (jnp.sum(give, axis=-1) <= jnp.sum(take, axis=-1)) & (jnp.max(moved, axis=(-2, -1)) <= MOVE)
    giver_at = top[..., None, None] + begin - give_from[..., :, None]
    taker_at = (top[..., None] - take - take_from)[..., None, :] + begin
    return moved, giver_at, taker_at, feasible


def lowest_top(counts, total):
    tops = FIXED + 4 * jnp.arange((total - FIXED) // 4 + 1, dtype=jnp.int32)
    _, _, _, feasible = flows(counts[None], jnp.broadcast_to(tops[:, None], (tops.shape[0], counts.shape[0])))
    return jnp.min(jnp.where(feasible, tops[:, None], total), axis=0).astype(jnp.int32)


def pack_kernel(split, front_slots, info, place, child, *refs):
    group, half = info[0], info[1]
    col_tiles = place.shape[0] // front_slots
    strips, in_sem, out_sem = refs[-3:]
    targets = [(0, split, refs[0], refs[1])]
    if len(refs) == 7:
        targets.append((split, place.shape[0] * 2, refs[2], refs[3]))

    def strip_in(j):
        slot = j % STRIPS
        row = pl.multiple_of((group + j) * BS, BS)
        return pltpu.make_async_copy(child.at[pl.ds(row, BS)], strips.at[slot], in_sem.at[slot])

    def tile_out(j, c, spot, kept_half, sent_half):
        slot = j % STRIPS
        col = pl.multiple_of(c * BS, BS)
        own = pl.multiple_of(half * HALF, HALF)
        other = pl.multiple_of((1 - half) * HALF, HALF)
        return (
            pltpu.make_async_copy(
                strips.at[slot, pl.ds(own, HALF), pl.ds(col, BS)], kept_half.at[spot], out_sem.at[0, slot]
            ),
            pltpu.make_async_copy(
                strips.at[slot, pl.ds(other, HALF), pl.ds(col, BS)], sent_half.at[spot], out_sem.at[1, slot]
            ),
        )

    def each_tile(j, act):
        def one(c, carry):
            spot = place[c * front_slots + j]

            for low, high, kept_half, sent_half in targets:

                @pl.when((spot >= low) & (spot < high))
                def _():
                    for copy in tile_out(j, c, spot - low, kept_half, sent_half):
                        act(copy)

            return carry

        lax.fori_loop(0, col_tiles, one, 0)

    for j in range(min(STRIPS - 1, front_slots)):
        strip_in(j).start()
    for j in range(front_slots):
        strip_in(j).wait()
        each_tile(j, lambda copy: copy.start())
        if j >= 1:
            each_tile(j - 1, lambda copy: copy.wait())
        if j + STRIPS - 1 < front_slots:
            strip_in(j + STRIPS - 1).start()
    each_tile(front_slots - 1, lambda copy: copy.wait())


def pack(child, info, place, sizes, front_slots):
    shapes = tuple(jax.ShapeDtypeStruct((size, HALF, BS), jnp.float32) for size in sizes for _ in range(2))
    smem = pl.BlockSpec(memory_space=pltpu.SMEM)
    hbm = pl.BlockSpec(memory_space=pl.ANY)
    return pl.pallas_call(
        functools.partial(pack_kernel, sizes[0], front_slots),
        out_shape=shapes,
        in_specs=[smem, smem, hbm],
        out_specs=(hbm,) * len(shapes),
        scratch_shapes=[
            pltpu.VMEM((STRIPS, BS, child.shape[1]), jnp.float32),
            pltpu.SemaphoreType.DMA((STRIPS,)),
            pltpu.SemaphoreType.DMA((2, STRIPS)),
        ],
        compiler_params=pltpu.CompilerParams(vmem_limit_bytes=VMEM_BYTES),
        cost_estimate=SMALL_COST,
        name="pack_tiles",
    )(info, place, child)


def tile_add_kernel(front_slots, info, listed, rows, acc_in, own, other, acc, held, part, done, in_sem, out_sem):
    begin, end, place, half = info[0], info[1], info[2], info[3]
    wide_count, narrow_index, narrow_count = info[4], info[5], info[6]

    def spot(i):
        k = listed[i]
        col_tile = k // front_slots
        row_block = rows[k % front_slots]
        row = pl.multiple_of(row_block // wide_count * BS, BS)
        col = pl.multiple_of(col_tile * BS, BS)
        global_tile = (col_tile // PIECES * narrow_count + narrow_index) * PIECES + col_tile % PIECES
        return row, col, row_block == global_tile

    def copies_in(i):
        slot = i % RING
        row, col, _ = spot(i)
        at = place + i
        mine = pl.multiple_of(half * HALF, HALF)
        its = pl.multiple_of((1 - half) * HALF, HALF)
        return (
            pltpu.make_async_copy(acc.at[pl.ds(row, BS), pl.ds(col, BS)], held.at[slot], in_sem.at[0, slot]),
            pltpu.make_async_copy(own.at[at], part.at[slot, pl.ds(mine, HALF)], in_sem.at[1, slot]),
            pltpu.make_async_copy(other.at[at], part.at[slot, pl.ds(its, HALF)], in_sem.at[2, slot]),
        )

    def copy_out(i):
        slot = i % RING
        row, col, _ = spot(i)
        return pltpu.make_async_copy(done.at[slot], acc.at[pl.ds(row, BS), pl.ds(col, BS)], out_sem.at[slot])

    def issue(i):
        @pl.when(i < end)
        def _():
            for copy in copies_in(i):
                copy.start()

    for ahead in range(RING - 1):
        issue(begin + ahead)

    def step(i, carry):
        issue(i + RING - 1)
        for copy in copies_in(i):
            copy.wait()

        @pl.when(i - RING >= begin)
        def _():
            copy_out(i - RING).wait()

        slot = i % RING
        _, _, diagonal = spot(i)
        below = lax.broadcasted_iota(jnp.int32, (BS, BS), 0) >= lax.broadcasted_iota(jnp.int32, (BS, BS), 1)
        total = held[slot] + part[slot]
        done[slot] = jnp.where(below | jnp.logical_not(diagonal), total, 0.0)
        copy_out(i).start()
        return carry

    lax.fori_loop(begin, end, step, 0)

    def drain(i, carry):
        copy_out(i).wait()
        return carry

    lax.fori_loop(jnp.maximum(begin, end - RING), end, drain, 0)


def tile_add(acc, own, other, info, listed, rows, front_slots):
    smem = pl.BlockSpec(memory_space=pltpu.SMEM)
    hbm = pl.BlockSpec(memory_space=pl.ANY)
    return pl.pallas_call(
        functools.partial(tile_add_kernel, front_slots),
        out_shape=jax.ShapeDtypeStruct(acc.shape, acc.dtype),
        in_specs=[smem, smem, smem, hbm, hbm, hbm],
        out_specs=hbm,
        scratch_shapes=[
            pltpu.VMEM((RING, BS, BS), jnp.float32),
            pltpu.VMEM((RING, BS, BS), jnp.float32),
            pltpu.VMEM((RING, BS, BS), jnp.float32),
            pltpu.SemaphoreType.DMA((3, RING)),
            pltpu.SemaphoreType.DMA((RING,)),
        ],
        input_output_aliases={3: 0},
        cost_estimate=SMALL_COST,
        name="add_tiles",
    )(info, listed, rows, acc, own, other)


def panel_base_kernel(kept_row, present, front, kept, mask, out):
    s = pl.program_id(0)
    take = (mask[...] > 0) & (present[s] > 0)
    out[...] = front[...] + jnp.where(take, kept[...], 0.0)


def panel_base(front, child, kept_row, present, mask):
    local_rows = front.shape[0]
    return pl.pallas_call(
        panel_base_kernel,
        out_shape=jax.ShapeDtypeStruct((local_rows, PW), jnp.float32),
        grid_spec=pltpu.PrefetchScalarGridSpec(
            num_scalar_prefetch=2,
            grid=(local_rows // BS,),
            in_specs=[
                pl.BlockSpec((BS, PW), lambda s, kept_row, present: (s, 0)),
                pl.BlockSpec((BS, PW), lambda s, kept_row, present: (kept_row[s], 0)),
                pl.BlockSpec((1, PW), lambda s, kept_row, present: (0, 0)),
            ],
            out_specs=pl.BlockSpec((BS, PW), lambda s, kept_row, present: (s, 0)),
        ),
        cost_estimate=SMALL_COST,
        name="panel_base",
    )(kept_row, present, front, child, mask)


def exact_dot(left, right, contract):
    return lax.dot_general(
        left, right, (contract, ((), ())), precision=HIGHEST_PRECISION, preferred_element_type=jnp.float32
    )


def factor_kernel(diag, lower, inverse, work, pair):
    size = diag.shape[0]
    full = diag[...]
    row = lax.broadcasted_iota(jnp.int32, (size, size), 0)
    col = lax.broadcasted_iota(jnp.int32, (size, size), 1)
    work[...] = jnp.where(row >= col, full, full.T)
    lower[...] = jnp.zeros_like(lower)
    inverse[...] = jnp.zeros_like(inverse)
    block_row = lax.broadcasted_iota(jnp.int32, (BS, BS), 0)
    block_col = lax.broadcasted_iota(jnp.int32, (BS, BS), 1)
    strip_row = lax.broadcasted_iota(jnp.int32, (STRIP, 2 * BS), 0)
    strip_lane = lax.broadcasted_iota(jnp.int32, (STRIP, 2 * BS), 1)
    for k in range(size // BS):
        here = slice(k * BS, (k + 1) * BS)
        pair[:, :BS] = work[here, here]
        pair[:, BS:] = jnp.where(block_row == block_col, 1.0, 0.0)

        def eliminate(step, carry):
            top = pl.multiple_of(step * STRIP, STRIP)
            strip = pair[pl.ds(top, STRIP), :]
            for j in range(STRIP):
                column = jnp.sum(jnp.where(strip_lane == top + j, strip, 0.0), axis=1, keepdims=True)
                scale = lax.rsqrt(column[j : j + 1])
                pivot = strip[j : j + 1] * scale
                reduced = strip - (column * scale) * pivot
                strip = jnp.where(strip_row > j, reduced, jnp.where(strip_row == j, pivot, strip))
            pair[pl.ds(top, STRIP), :] = strip
            ahead = jnp.where(strip_lane[:, :BS] >= top + STRIP, strip[:, :BS], 0.0)
            pair[...] -= exact_dot(ahead.T, strip, ((1,), (0,)))
            return carry

        lax.fori_loop(0, BS // STRIP, eliminate, 0)
        own_inverse = jnp.where(block_row >= block_col, pair[:, BS:], 0.0)
        lower[here, here] = jnp.where(block_row <= block_col, pair[:, :BS], 0.0).T
        inverse[here, here] = own_inverse
        if (k + 1) * BS < size:
            below = slice((k + 1) * BS, size)
            column_block = exact_dot(work[below, here], own_inverse, ((1,), (1,)))
            lower[below, here] = column_block
            work[below, below] -= exact_dot(column_block, column_block, ((1,), (1,)))
        if k:
            before = slice(0, k * BS)
            product = exact_dot(lower[here, before], inverse[before, before], ((1,), (0,)))
            inverse[here, before] = -exact_dot(own_inverse, product, ((1,), (0,)))


def factor_block(diag):
    shape = jax.ShapeDtypeStruct(diag.shape, jnp.float32)
    return pl.pallas_call(
        factor_kernel,
        out_shape=(shape, shape),
        scratch_shapes=[pltpu.VMEM(diag.shape, jnp.float32), pltpu.VMEM((BS, 2 * BS), jnp.float32)],
        compiler_params=pltpu.CompilerParams(vmem_limit_bytes=VMEM_BYTES),
        cost_estimate=SMALL_COST,
        name="factor_block",
    )(diag)


def solve_kernel(with_diagonal, where, rows, inverse, lower, out):
    out[...] = exact_dot(rows[...], inverse[...], ((1,), (1,)))
    if with_diagonal:
        wide_index, wide_count = where[0], where[1]
        for part in range(rows.shape[0] // BS):
            row_block = (pl.program_id(0) * ROW_GROUP + part) * wide_count + wide_index

            @pl.when(row_block < PIECES)
            def _():
                start = pl.multiple_of(row_block * BS, BS)
                out[part * BS : (part + 1) * BS, :] = lower[pl.ds(start, BS), :]


def solve(rows, inverse, lower, where, with_diagonal):
    tall = ROW_GROUP * BS
    whole = pl.BlockSpec((PW, PW), lambda g, where: (0, 0))
    strip = pl.BlockSpec((tall, PW), lambda g, where: (g, 0))
    return pl.pallas_call(
        functools.partial(solve_kernel, with_diagonal),
        out_shape=jax.ShapeDtypeStruct(rows.shape, jnp.float32),
        grid_spec=pltpu.PrefetchScalarGridSpec(
            num_scalar_prefetch=1,
            grid=(rows.shape[0] // tall,),
            in_specs=[strip, whole, whole],
            out_specs=strip,
        ),
        compiler_params=pltpu.CompilerParams(vmem_limit_bytes=VMEM_BYTES),
        cost_estimate=SMALL_COST,
        name="solve_rows",
    )(where, rows, inverse, lower)


def update_kernel(kept_row, present, where, front, kept0, kept1, kept2, kept3, mask, factor, rhs, out, rhs_high, rhs_low):
    g = pl.program_id(0)

    @pl.when(g == 0)
    def _():
        rhs_high[...] = rhs[...].astype(jnp.bfloat16)
        rhs_low[...] = (rhs[...] - rhs_high[...].astype(jnp.float32)).astype(jnp.bfloat16)

    wide_index, wide_count, narrow_index, narrow_count = where[0], where[1], where[2], where[3]
    left = factor[...]
    left_high = left.astype(jnp.bfloat16)
    left_low = (left - left_high.astype(jnp.float32)).astype(jnp.bfloat16)
    rows = left.shape[0]
    col_slots = out.shape[1] // PW
    row_local = lax.broadcasted_iota(jnp.int32, (rows, PW), 0)
    slot = g * ROW_GROUP + row_local // BS
    global_row = (slot * wide_count + wide_index) * BS + row_local % BS
    col_in_block = lax.broadcasted_iota(jnp.int32, (rows, PW), 1)
    dims = (((1,), (1,)), ((), ()))
    for t in range(col_slots):
        cols = pl.ds(t * PW, PW)
        column_block = t * narrow_count + narrow_index
        high = rhs_high[cols, :]
        low = rhs_low[cols, :]
        product = lax.dot_general(left_high, high, dims, preferred_element_type=jnp.float32)
        product += lax.dot_general(left_high, low, dims, preferred_element_type=jnp.float32)
        product += lax.dot_general(left_low, high, dims, preferred_element_type=jnp.float32)
        below = global_row >= column_block * PW + col_in_block
        take = mask[:, cols] > 0
        for part, kept in enumerate((kept0, kept1, kept2, kept3)):
            rows_here = slice(part * BS, (part + 1) * BS)
            there = take & (present[g * ROW_GROUP + part] > 0)
            base = front[rows_here, cols] + jnp.where(there, kept[:, cols], 0.0)
            value = base - product[rows_here]
            if t == 0:
                value = jnp.where(column_block > 0, value, left[rows_here])
            out[rows_here, cols] = jnp.where(below[rows_here], value, 0.0)


def update(front, child, kept_row, present, where, mask, factor, rhs):
    local_rows, local_cols = front.shape
    tall = ROW_GROUP * BS

    def kept_spec(part):
        return pl.BlockSpec(
            (BS, local_cols), lambda g, kept_row, present, where: (kept_row[g * ROW_GROUP + part], 0)
        )

    def fixed(shape):
        return pl.BlockSpec(shape, lambda g, kept_row, present, where: (0, 0))

    def tall_spec(width):
        return pl.BlockSpec((tall, width), lambda g, kept_row, present, where: (g, 0))

    return pl.pallas_call(
        update_kernel,
        out_shape=jax.ShapeDtypeStruct(front.shape, jnp.float32),
        grid_spec=pltpu.PrefetchScalarGridSpec(
            num_scalar_prefetch=3,
            grid=(local_rows // tall,),
            in_specs=[tall_spec(local_cols)]
            + [kept_spec(part) for part in range(ROW_GROUP)]
            + [
                fixed((1, local_cols)),
                tall_spec(PW),
                fixed((local_cols, PW)),
            ],
            out_specs=tall_spec(local_cols),
            scratch_shapes=[
                pltpu.VMEM((local_cols, PW), jnp.bfloat16),
                pltpu.VMEM((local_cols, PW), jnp.bfloat16),
            ],
        ),
        compiler_params=pltpu.CompilerParams(vmem_limit_bytes=VMEM_BYTES),
        cost_estimate=SMALL_COST,
        name="trailing_update",
    )(kept_row, present, where, front, child, child, child, child, mask, factor, rhs)


def shards(front, child_update, child_map):
    wide_count = lax.axis_size("wide")
    narrow_count = lax.axis_size("narrow")
    wide_index = lax.axis_index("wide")
    narrow_index = lax.axis_index("narrow")
    half_count = wide_count // 2
    local_rows, local_cols = front.shape
    front_slots = local_rows // BS
    col_slots = local_cols // PW
    col_tiles = local_cols // BS
    block_total = front_slots * wide_count
    child_side = wide_index // half_count
    partner = wide_index ^ half_count
    core = narrow_index % 2
    total = 2 * front_slots * col_tiles

    _, send_need = tile_tables(child_map, wide_index, front_slots, col_tiles)
    got_rows, got_need = tile_tables(child_map, partner, front_slots, col_tiles)
    send_counts = jnp.sum(send_need, axis=1).astype(jnp.int32)
    got_counts = jnp.sum(got_need, axis=1).astype(jnp.int32)
    own_need = jnp.where(core == 0, send_need[0], send_need[1])
    got_list = sending_list(jnp.where(core == 0, got_need[0], got_need[1]))
    send_base = jnp.where(core == 0, 0, send_counts[0])
    send_place = jnp.where(own_need, send_base + ranks(own_need), -1).astype(jnp.int32)
    got_base = jnp.where(core == 0, 0, got_counts[0])
    got_count = jnp.where(core == 0, got_counts[0], got_counts[1])
    pack_info = jnp.stack([(1 - child_side) * front_slots, core]).astype(jnp.int32)

    head_split = min(HEAD, total)
    has_more = total > HEAD

    def joined(kept_half, swapped, low):
        at = low + jnp.arange(kept_half.shape[0], dtype=jnp.int32)
        is_own = (at >= send_counts[0]) == (core == 1)
        return jnp.where(is_own[:, None, None], kept_half, swapped)

    room = total - head_split + LATE
    packed = pack(
        child_update, pack_info, send_place, [head_split, room] if has_more else [head_split], front_slots
    )
    head = joined(packed[0], core_swap(packed[1]), 0)
    first_split = min(FIRST, head_split)
    heads = [(0, first_split, cross(head[:first_split], half_count))]
    second = head[first_split:]
    if has_more:
        counts = lax.dynamic_index_in_dim(
            chip_counts(child_map, front_slots, col_tiles), narrow_index // 2, 1, keepdims=False
        )
        counts = jnp.maximum(counts, FIXED).reshape(wide_count // QUAD, QUAD)
        tops = lowest_top(counts, total)
        moved, giver_at, taker_at, _ = flows(counts, tops)
        send_top = tops[wide_index // QUAD]
        got_top = tops[partner // QUAD]
        member = wide_index % QUAD
        send_quad = (moved[wide_index // QUAD], giver_at[wide_index // QUAD], taker_at[wide_index // QUAD])
        got_quad = (moved[partner // QUAD], giver_at[partner // QUAD], taker_at[partner // QUAD])

        rest = joined(packed[2], core_swap(packed[3]), head_split)
        soon = rest[: SOON - head_split]

        given = [
            lax.dynamic_slice_in_dim(rest, send_quad[1][member, member ^ mask] - head_split, MOVE)
            for mask in range(1, QUAD)
        ]
        second, soon, given, rest = lax.optimization_barrier((second, soon, given, rest))
        taken = [cross(given[mask - 1], mask) for mask in range(1, QUAD)]
    if first_split < head_split:
        heads.append((first_split, head_split, cross(second, half_count)))

    own_map = lax.dynamic_slice_in_dim(child_map, (wide_index * 2 + child_side) * front_slots, front_slots)
    target = wide_index + wide_count * jnp.arange(front_slots, dtype=jnp.int32)
    kept_hit = own_map[None, :] == target[:, None]
    present = jnp.any(kept_hit, axis=1).astype(jnp.int32)
    kept_slot = jnp.sum(jnp.where(kept_hit, jnp.arange(front_slots, dtype=jnp.int32)[None, :], 0), axis=1)
    kept_row = (child_side * front_slots + kept_slot).astype(jnp.int32)
    col_local = jnp.arange(local_cols, dtype=jnp.int32)
    global_col = (col_local // PW * narrow_count + narrow_index) * PW + col_local % PW
    names = lax.dynamic_slice_in_dim(child_map, child_side * block_total, block_total)
    named_cols = jnp.any(names[:, None] == (global_col // BS)[None, :], axis=0).astype(jnp.int32)[None, :]
    panel = panel_base(front, child_update, kept_row, present, named_cols[:, :PW])

    if has_more:
        got_soon = cross(soon, half_count)

    panel_count = jnp.where(
        narrow_index == 0, jnp.sum(got_need[0, : PIECES * front_slots]).astype(jnp.int32), 0
    )

    def add(matrix, tiles, first, last, low, high, other=None):
        begin = jnp.maximum(jnp.maximum(low - got_base, 0), first)
        end = jnp.minimum(jnp.minimum(high - got_base, got_count), last)
        info = jnp.stack(
            [
                begin,
                jnp.maximum(begin, end),
                got_base - low,
                core,
                jnp.int32(wide_count),
                narrow_index,
                jnp.int32(narrow_count),
            ]
        ).astype(jnp.int32)
        other = core_swap(tiles) if other is None else other
        return tile_add(matrix, tiles, other, info, got_list, got_rows, front_slots)

    heads[0] += (core_swap(heads[0][2]),)
    if has_more:
        second, taken, first = lax.optimization_barrier((heads[1][2], taken, heads[0][3]))
        heads = [heads[0][:3] + (first,), heads[1][:2] + (second, core_swap(second))]
    for low, high, tiles, other in heads:
        panel = add(panel, tiles, 0, panel_count, low, high, other)
    if has_more:
        panel, got_soon = lax.optimization_barrier((panel, got_soon))
        got_next = cross(rest[SOON - head_split : NEXT - head_split], half_count)
    panel = from_first(panel)

    window = local_cols * narrow_count
    window_slots = max(1, window // (BS * wide_count))
    pieces = far_pieces(panel[: window_slots * BS])
    if has_more:
        relayed = rest
        for mask in range(1, QUAD):
            at = send_quad[2][member ^ mask, member] - head_split
            kept_there = lax.dynamic_slice_in_dim(relayed, at, MOVE)
            valid = jnp.arange(MOVE, dtype=jnp.int32) < send_quad[0][member ^ mask, member]
            relayed = lax.dynamic_update_slice_in_dim(
                relayed, jnp.where(valid[:, None, None], taken[mask - 1], kept_there), at, 0
            )
        send_late = jnp.maximum(send_top - LATE, FIXED)
        got_late = jnp.maximum(got_top - LATE, FIXED)
        late = lax.dynamic_slice_in_dim(relayed, send_late - head_split, LATE)
        late, pieces, got_next = lax.optimization_barrier((late, pieces, got_next))
        got_late_tiles = cross(late, half_count)

    gathered = near_pieces(pieces)
    diag_half = gathered[0, 0].reshape(PW, PW // 2)
    by_rows = gathered.reshape(-1, PW // 2)[:window].reshape(col_slots, narrow_count, PW, PW // 2)

    def whole_rows(mine, others):
        return jnp.where(
            core == 0, jnp.concatenate([mine, others], 1), jnp.concatenate([others, mine], 1)
        )

    def rows_of(index):
        return lax.dynamic_index_in_dim(by_rows, index, 1, keepdims=False).reshape(local_cols, PW // 2)

    diag_block = whole_rows(diag_half, core_swap(diag_half))
    if has_more:
        body = rest[NEXT - head_split : FIXED - head_split]
        diag_block, body = lax.optimization_barrier((diag_block, body))
        got_body = cross(body, half_count)
    raw_rows = whole_rows(rows_of(narrow_index), core_swap(rows_of(narrow_index ^ 1)))
    factor_diag, inverse = factor_block(diag_block)
    if has_more:
        inverse, got_late_tiles = lax.optimization_barrier((inverse, got_late_tiles))
        padded = jnp.concatenate([got_late_tiles, jnp.zeros_like(got_late_tiles[:MOVE])], 0)
        given_back = [
            lax.dynamic_slice_in_dim(padded, got_quad[2][member ^ mask, member] - got_late, MOVE)
            for mask in range(1, QUAD)
        ]
        inverse, given_back = lax.optimization_barrier((inverse, given_back))
        returned = [cross(given_back[mask - 1], mask) for mask in range(1, QUAD)]

    where = jnp.stack(
        [wide_index, jnp.int32(wide_count), narrow_index, jnp.int32(narrow_count)]
    ).astype(jnp.int32)
    factor = solve(panel, inverse, factor_diag, where, True)
    panel_rows = solve(raw_rows, inverse, factor_diag, where, False)
    matrix = update(front, child_update, kept_row, present, where, named_cols, factor, panel_rows)

    for low, high, tiles, other in heads:
        matrix = add(matrix, tiles, panel_count, total, low, high, other)
    if has_more:
        matrix = add(matrix, got_soon, panel_count, total, head_split, SOON)
        matrix = add(matrix, got_late_tiles, panel_count, total, got_late, got_top)
        matrix = add(matrix, got_next, panel_count, total, SOON, NEXT)
        matrix, got_body, returned = lax.optimization_barrier((matrix, got_body, returned))
        steps = jnp.maximum((jnp.max(tops) - LATE - FIXED + CHUNK - 1) // CHUNK, 1)

        def add_held(matrix):
            matrix = add(matrix, got_body, panel_count, total, NEXT, FIXED)
            for mask in range(1, QUAD):
                low = got_quad[1][member, member ^ mask]
                high = low + got_quad[0][member, member ^ mask]
                matrix = add(matrix, returned[mask - 1], panel_count, total, low, high)
            return matrix

        def add_chunk(matrix, tiles, i):
            low = FIXED + (i - 1) * CHUNK
            return add(matrix, tiles, panel_count, total, low, jnp.minimum(low + CHUNK, got_late))

        def tail(i, carried):
            matrix, tiles = carried
            low = FIXED + i * CHUNK
            got = cross(lax.dynamic_slice_in_dim(relayed, low - head_split, CHUNK), half_count)
            matrix = lax.cond(i == 0, add_held, lambda matrix: add_chunk(matrix, tiles, i), matrix)
            return matrix, got

        matrix, last = lax.fori_loop(0, steps, tail, (matrix, got_body[:CHUNK]))
        matrix = add_chunk(matrix, last, steps)
    return matrix


def solution(mesh):
    placed = (P("wide", "narrow"), P("wide", "narrow"), P())
    return jax.shard_map(
        shards, mesh=mesh, in_specs=placed, out_specs=P("wide", "narrow"), check_vma=False
    )
```

```python
import functools

import jax
import jax.numpy as jnp
import numpy as np
from jax import lax
from jax.experimental import pallas as pl
from jax.experimental.pallas import tpu as pltpu
from jax.sharding import PartitionSpec as P

BS = 128
PW = 512
HALF = BS // 2
PIECES = PW // BS
FIRST = 40
HEAD = 88
SOON = 112
NEXT = 136
FIXED = 200
LATE = 96
MOVES = (64, 64, 40)
CHUNK = 16
QUAD = 4
STRIP = 8
STRIPS = 4
RING = 8
ROW_GROUP = 4
VMEM_BYTES = 56 * 1024 * 1024
SMALL_COST = pl.CostEstimate(flops=1024, bytes_accessed=1024, transcendentals=0)

HIGHEST_PRECISION = lax.Precision.HIGHEST


def cross(value, half_count):
    size = lax.axis_size("wide")
    return lax.ppermute(value, "wide", [(i, i ^ half_count) for i in range(size)])


def cross_first_core(value, half_count):
    narrow = lax.axis_size("narrow")
    size = lax.axis_size("wide") * narrow
    pairs = [(i, i ^ half_count * narrow) for i in range(0, size, 2)]
    return lax.ppermute(value, ("wide", "narrow"), pairs)


def core_swap(value):
    size = lax.axis_size("narrow")
    return lax.ppermute(value, "narrow", [(i, i ^ 1) for i in range(size)])


def from_first(value):
    size = lax.axis_size("narrow")
    if size == 2:
        moved = lax.ppermute(value, "narrow", [(0, 1)])
        return jnp.where(lax.axis_index("narrow") == 0, value, moved)
    mine = jnp.where(lax.axis_index("narrow") == 0, value, jnp.zeros_like(value))
    return lax.psum(mine, "narrow")


def far_pieces(piece):
    wide_count = lax.axis_size("wide")
    half_cols = piece.shape[1] // 2
    mine = lax.dynamic_slice_in_dim(piece, lax.axis_index("narrow") % 2 * half_cols, half_cols, 1)
    return [mine] + [cross(mine, mask) for mask in range(QUAD, wide_count, QUAD)]


def near_pieces(pieces):
    wide_index = lax.axis_index("wide")
    far = jnp.stack(pieces)
    quads, rows, half_cols = far.shape
    each = jnp.stack([far] + [cross(far, mask) for mask in range(1, QUAD)])
    bits = (QUAD * quads).bit_length() - 1
    each = each.reshape((2,) * bits + (rows, half_cols))
    masks = [QUAD >> shift for shift in range(1, QUAD.bit_length())]
    masks += [(QUAD * quads) >> shift for shift in range(1, quads.bit_length())]
    for axis, mask in enumerate(masks):
        each = jnp.where(wide_index // mask % 2 == 1, jnp.flip(each, axis), each)
    each = each.reshape(QUAD, quads, rows // BS, BS, half_cols)
    return each.transpose(2, 1, 0, 3, 4)


def tile_tables(child_map, source, front_slots, col_tiles):
    wide_count = lax.axis_size("wide")
    narrow_count = lax.axis_size("narrow")
    block_total = front_slots * wide_count
    side = source // (wide_count // 2)
    rows = lax.dynamic_slice_in_dim(child_map, (source * 2 + 1 - side) * front_slots, front_slots)
    names = lax.dynamic_slice_in_dim(child_map, side * block_total, block_total)
    tiles = jnp.arange(col_tiles, dtype=jnp.int32)
    first_core = lax.axis_index("narrow") // 2 * 2
    cores = first_core + jnp.arange(2, dtype=jnp.int32)
    global_tile = (tiles[None] // PIECES * narrow_count + cores[:, None]) * PIECES + tiles[None] % PIECES
    named = jnp.any(names[None, None, :] == global_tile[:, :, None], axis=2)
    need = named[:, :, None] & (rows[None, None, :] >= global_tile[:, :, None])
    need = need.reshape(2, col_tiles * front_slots)
    return rows, need


def chip_counts(child_map, front_slots, col_tiles):
    wide_count = lax.axis_size("wide")
    narrow_count = lax.axis_size("narrow")
    sides = jnp.arange(wide_count, dtype=jnp.int32) // (wide_count // 2)
    rows = child_map.reshape(wide_count, 2, front_slots)
    rows = jnp.where((sides == 0)[:, None], rows[:, 1], rows[:, 0])
    names = child_map.reshape(2, front_slots * wide_count)
    tiles = jnp.arange(col_tiles * narrow_count, dtype=jnp.int32)
    named = jnp.any(names[:, None, :] == tiles[None, :, None], axis=2)
    named = jnp.where((sides == 0)[:, None], named[:1], named[1:])
    each = jnp.sum(named[:, None, :] & (rows[:, :, None] >= tiles[None, None, :]), axis=1).astype(jnp.int32)
    each = each.reshape(wide_count, col_tiles // PIECES, narrow_count // 2, 2, PIECES)
    each = jnp.sum(each, axis=(1, 4))
    return jnp.maximum(each[..., 0], min(FIRST, front_slots * col_tiles)) + each[..., 1]


def ranks(need):
    order = jnp.arange(need.shape[0], dtype=jnp.int32)
    return jnp.sum((order[None, :] < order[:, None]) & need[None, :], axis=1).astype(jnp.int32)


def sending_list(need):
    order = jnp.arange(need.shape[0], dtype=jnp.int32)
    hit = (ranks(need)[None, :] == order[:, None]) & need[None, :]
    return jnp.sum(jnp.where(hit, order[None, :], 0), axis=1).astype(jnp.int32)


def flows(counts, top):
    give = jnp.maximum(counts - top[..., None], 0)
    take = jnp.clip(top[..., None] - counts, 0, LATE)
    give_from = jnp.cumsum(give, axis=-1) - give
    take_from = jnp.cumsum(take, axis=-1) - take
    begin = jnp.maximum(give_from[..., :, None], take_from[..., None, :])
    end = jnp.minimum((give_from + give)[..., :, None], (take_from + take)[..., None, :])
    moved = jnp.maximum(end - begin, 0)
    chips = np.arange(QUAD)
    limits = np.array((0,) + MOVES)[chips[:, None] ^ chips[None, :]]
    feasible = (jnp.sum(give, axis=-1) <= jnp.sum(take, axis=-1)) & jnp.all(moved <= limits, axis=(-2, -1))
    giver_at = top[..., None, None] + begin - give_from[..., :, None]
    taker_at = (top[..., None] - take - take_from)[..., None, :] + begin
    return moved, giver_at, taker_at, feasible


def lowest_top(counts, total):
    tops = FIXED + 4 * jnp.arange((total - FIXED) // 4 + 1, dtype=jnp.int32)
    _, _, _, feasible = flows(counts[None], jnp.broadcast_to(tops[:, None], (tops.shape[0], counts.shape[0])))
    return jnp.min(jnp.where(feasible, tops[:, None], total), axis=0).astype(jnp.int32)


def pack_kernel(bounds, front_slots, info, place, child, *refs):
    group, half = info[0], info[1]
    col_tiles = place.shape[0] // front_slots
    strips, in_sem, out_sem = refs[-3:]
    targets = [(0, bounds[1], refs[0], refs[0], bounds[1])]
    for part, (low, high) in enumerate(zip(bounds[1:], bounds[2:])):
        targets.append((low, high, refs[2 * part + 1], refs[2 * part + 2], 0))

    def strip_in(j):
        slot = j % STRIPS
        row = pl.multiple_of((group + j) * BS, BS)
        return pltpu.make_async_copy(child.at[pl.ds(row, BS)], strips.at[slot], in_sem.at[slot])

    def tile_out(j, c, spot, kept_half, sent_half, later):
        slot = j % STRIPS
        col = pl.multiple_of(c * BS, BS)
        own = pl.multiple_of(half * HALF, HALF)
        other = pl.multiple_of((1 - half) * HALF, HALF)
        return (
            pltpu.make_async_copy(
                strips.at[slot, pl.ds(own, HALF), pl.ds(col, BS)], kept_half.at[spot], out_sem.at[0, slot]
            ),
            pltpu.make_async_copy(
                strips.at[slot, pl.ds(other, HALF), pl.ds(col, BS)], sent_half.at[later + spot], out_sem.at[1, slot]
            ),
        )

    def each_tile(j, act):
        def one(c, carry):
            spot = place[c * front_slots + j]

            for low, high, kept_half, sent_half, later in targets:

                @pl.when((spot >= low) & (spot < high))
                def _():
                    for copy in tile_out(j, c, spot - low, kept_half, sent_half, later):
                        act(copy)

            return carry

        lax.fori_loop(0, col_tiles, one, 0)

    for j in range(min(STRIPS - 1, front_slots)):
        strip_in(j).start()
    for j in range(front_slots):
        strip_in(j).wait()
        each_tile(j, lambda copy: copy.start())
        if j >= 1:
            each_tile(j - 1, lambda copy: copy.wait())
        if j + STRIPS - 1 < front_slots:
            strip_in(j + STRIPS - 1).start()
    each_tile(front_slots - 1, lambda copy: copy.wait())


def pack(child, info, place, bounds, room, front_slots):
    sizes = [high - low for low, high in zip(bounds[1:], bounds[2:])]
    sizes[-1] += room
    sizes = [2 * bounds[1]] + [size for size in sizes for _ in range(2)]
    shapes = tuple(jax.ShapeDtypeStruct((size, HALF, BS), jnp.float32) for size in sizes)
    smem = pl.BlockSpec(memory_space=pltpu.SMEM)
    hbm = pl.BlockSpec(memory_space=pl.ANY)
    return pl.pallas_call(
        functools.partial(pack_kernel, tuple(bounds), front_slots),
        out_shape=shapes,
        in_specs=[smem, smem, hbm],
        out_specs=(hbm,) * len(shapes),
        scratch_shapes=[
            pltpu.VMEM((STRIPS, BS, child.shape[1]), jnp.float32),
            pltpu.SemaphoreType.DMA((STRIPS,)),
            pltpu.SemaphoreType.DMA((2, STRIPS)),
        ],
        compiler_params=pltpu.CompilerParams(vmem_limit_bytes=VMEM_BYTES),
        cost_estimate=SMALL_COST,
        name="pack_tiles",
    )(info, place, child)


def tile_add_kernel(front_slots, info, listed, rows, acc_in, own, other, acc, held, part, done, in_sem, out_sem):
    begin, end, place, half = info[0], info[1], info[2], info[3]
    wide_count, narrow_index, narrow_count = info[4], info[5], info[6]

    def spot(i):
        k = listed[i]
        col_tile = k // front_slots
        row_block = rows[k % front_slots]
        row = pl.multiple_of(row_block // wide_count * BS, BS)
        col = pl.multiple_of(col_tile * BS, BS)
        global_tile = (col_tile // PIECES * narrow_count + narrow_index) * PIECES + col_tile % PIECES
        return row, col, row_block == global_tile

    def copies_in(i):
        slot = i % RING
        row, col, _ = spot(i)
        at = place + i
        mine = pl.multiple_of(half * HALF, HALF)
        its = pl.multiple_of((1 - half) * HALF, HALF)
        return (
            pltpu.make_async_copy(acc.at[pl.ds(row, BS), pl.ds(col, BS)], held.at[slot], in_sem.at[0, slot]),
            pltpu.make_async_copy(own.at[at], part.at[slot, pl.ds(mine, HALF)], in_sem.at[1, slot]),
            pltpu.make_async_copy(other.at[at], part.at[slot, pl.ds(its, HALF)], in_sem.at[2, slot]),
        )

    def copy_out(i):
        slot = i % RING
        row, col, _ = spot(i)
        return pltpu.make_async_copy(done.at[slot], acc.at[pl.ds(row, BS), pl.ds(col, BS)], out_sem.at[slot])

    def issue(i):
        @pl.when(i < end)
        def _():
            for copy in copies_in(i):
                copy.start()

    for ahead in range(RING - 1):
        issue(begin + ahead)

    def step(i, carry):
        issue(i + RING - 1)
        for copy in copies_in(i):
            copy.wait()

        @pl.when(i - RING >= begin)
        def _():
            copy_out(i - RING).wait()

        slot = i % RING
        _, _, diagonal = spot(i)
        below = lax.broadcasted_iota(jnp.int32, (BS, BS), 0) >= lax.broadcasted_iota(jnp.int32, (BS, BS), 1)
        total = held[slot] + part[slot]
        done[slot] = jnp.where(below | jnp.logical_not(diagonal), total, 0.0)
        copy_out(i).start()
        return carry

    lax.fori_loop(begin, end, step, 0)

    def drain(i, carry):
        copy_out(i).wait()
        return carry

    lax.fori_loop(jnp.maximum(begin, end - RING), end, drain, 0)


def tile_add(acc, own, other, info, listed, rows, front_slots):
    smem = pl.BlockSpec(memory_space=pltpu.SMEM)
    hbm = pl.BlockSpec(memory_space=pl.ANY)
    return pl.pallas_call(
        functools.partial(tile_add_kernel, front_slots),
        out_shape=jax.ShapeDtypeStruct(acc.shape, acc.dtype),
        in_specs=[smem, smem, smem, hbm, hbm, hbm],
        out_specs=hbm,
        scratch_shapes=[
            pltpu.VMEM((RING, BS, BS), jnp.float32),
            pltpu.VMEM((RING, BS, BS), jnp.float32),
            pltpu.VMEM((RING, BS, BS), jnp.float32),
            pltpu.SemaphoreType.DMA((3, RING)),
            pltpu.SemaphoreType.DMA((RING,)),
        ],
        input_output_aliases={3: 0},
        cost_estimate=SMALL_COST,
        name="add_tiles",
    )(info, listed, rows, acc, own, other)


def panel_base_kernel(kept_row, present, front, kept, mask, out):
    s = pl.program_id(0)
    take = (mask[...] > 0) & (present[s] > 0)
    out[...] = front[...] + jnp.where(take, kept[...], 0.0)


def panel_base(front, child, kept_row, present, mask):
    local_rows = front.shape[0]
    return pl.pallas_call(
        panel_base_kernel,
        out_shape=jax.ShapeDtypeStruct((local_rows, PW), jnp.float32),
        grid_spec=pltpu.PrefetchScalarGridSpec(
            num_scalar_prefetch=2,
            grid=(local_rows // BS,),
            in_specs=[
                pl.BlockSpec((BS, PW), lambda s, kept_row, present: (s, 0)),
                pl.BlockSpec((BS, PW), lambda s, kept_row, present: (kept_row[s], 0)),
                pl.BlockSpec((1, PW), lambda s, kept_row, present: (0, 0)),
            ],
            out_specs=pl.BlockSpec((BS, PW), lambda s, kept_row, present: (s, 0)),
        ),
        cost_estimate=SMALL_COST,
        name="panel_base",
    )(kept_row, present, front, child, mask)


def exact_dot(left, right, contract):
    return lax.dot_general(
        left, right, (contract, ((), ())), precision=HIGHEST_PRECISION, preferred_element_type=jnp.float32
    )


def factor_kernel(diag, lower, inverse, work, pair):
    size = diag.shape[0]
    full = diag[...]
    row = lax.broadcasted_iota(jnp.int32, (size, size), 0)
    col = lax.broadcasted_iota(jnp.int32, (size, size), 1)
    work[...] = jnp.where(row >= col, full, full.T)
    lower[...] = jnp.zeros_like(lower)
    inverse[...] = jnp.zeros_like(inverse)
    block_row = lax.broadcasted_iota(jnp.int32, (BS, BS), 0)
    block_col = lax.broadcasted_iota(jnp.int32, (BS, BS), 1)
    strip_row = lax.broadcasted_iota(jnp.int32, (STRIP, 2 * BS), 0)
    strip_lane = lax.broadcasted_iota(jnp.int32, (STRIP, 2 * BS), 1)
    for k in range(size // BS):
        here = slice(k * BS, (k + 1) * BS)
        pair[:, :BS] = work[here, here]
        pair[:, BS:] = jnp.where(block_row == block_col, 1.0, 0.0)

        def eliminate(step, carry):
            top = pl.multiple_of(step * STRIP, STRIP)
            strip = pair[pl.ds(top, STRIP), :]
            for j in range(STRIP):
                column = jnp.sum(jnp.where(strip_lane == top + j, strip, 0.0), axis=1, keepdims=True)
                scale = lax.rsqrt(column[j : j + 1])
                pivot = strip[j : j + 1] * scale
                reduced = strip - (column * scale) * pivot
                strip = jnp.where(strip_row > j, reduced, jnp.where(strip_row == j, pivot, strip))
            pair[pl.ds(top, STRIP), :] = strip
            ahead = jnp.where(strip_lane[:, :BS] >= top + STRIP, strip[:, :BS], 0.0)
            pair[...] -= exact_dot(ahead.T, strip, ((1,), (0,)))
            return carry

        lax.fori_loop(0, BS // STRIP, eliminate, 0)
        own_inverse = jnp.where(block_row >= block_col, pair[:, BS:], 0.0)
        lower[here, here] = jnp.where(block_row <= block_col, pair[:, :BS], 0.0).T
        inverse[here, here] = own_inverse
        if (k + 1) * BS < size:
            below = slice((k + 1) * BS, size)
            column_block = exact_dot(work[below, here], own_inverse, ((1,), (1,)))
            lower[below, here] = column_block
            work[below, below] -= exact_dot(column_block, column_block, ((1,), (1,)))
        if k:
            before = slice(0, k * BS)
            product = exact_dot(lower[here, before], inverse[before, before], ((1,), (0,)))
            inverse[here, before] = -exact_dot(own_inverse, product, ((1,), (0,)))


def factor_block(diag):
    shape = jax.ShapeDtypeStruct(diag.shape, jnp.float32)
    return pl.pallas_call(
        factor_kernel,
        out_shape=(shape, shape),
        scratch_shapes=[pltpu.VMEM(diag.shape, jnp.float32), pltpu.VMEM((BS, 2 * BS), jnp.float32)],
        compiler_params=pltpu.CompilerParams(vmem_limit_bytes=VMEM_BYTES),
        cost_estimate=SMALL_COST,
        name="factor_block",
    )(diag)


def solve_kernel(with_diagonal, where, rows, inverse, lower, out):
    out[...] = exact_dot(rows[...], inverse[...], ((1,), (1,)))
    if with_diagonal:
        wide_index, wide_count = where[0], where[1]
        for part in range(rows.shape[0] // BS):
            row_block = (pl.program_id(0) * ROW_GROUP + part) * wide_count + wide_index

            @pl.when(row_block < PIECES)
            def _():
                start = pl.multiple_of(row_block * BS, BS)
                out[part * BS : (part + 1) * BS, :] = lower[pl.ds(start, BS), :]


def solve(rows, inverse, lower, where, with_diagonal):
    tall = ROW_GROUP * BS
    whole = pl.BlockSpec((PW, PW), lambda g, where: (0, 0))
    strip = pl.BlockSpec((tall, PW), lambda g, where: (g, 0))
    return pl.pallas_call(
        functools.partial(solve_kernel, with_diagonal),
        out_shape=jax.ShapeDtypeStruct(rows.shape, jnp.float32),
        grid_spec=pltpu.PrefetchScalarGridSpec(
            num_scalar_prefetch=1,
            grid=(rows.shape[0] // tall,),
            in_specs=[strip, whole, whole],
            out_specs=strip,
        ),
        compiler_params=pltpu.CompilerParams(vmem_limit_bytes=VMEM_BYTES),
        cost_estimate=SMALL_COST,
        name="solve_rows",
    )(where, rows, inverse, lower)


def update_kernel(kept_row, present, where, front, kept0, kept1, kept2, kept3, mask, factor, rhs, out, rhs_high, rhs_low):
    g = pl.program_id(0)

    @pl.when(g == 0)
    def _():
        rhs_high[...] = rhs[...].astype(jnp.bfloat16)
        rhs_low[...] = (rhs[...] - rhs_high[...].astype(jnp.float32)).astype(jnp.bfloat16)

    wide_index, wide_count, narrow_index, narrow_count = where[0], where[1], where[2], where[3]
    left = factor[...]
    left_high = left.astype(jnp.bfloat16)
    left_low = (left - left_high.astype(jnp.float32)).astype(jnp.bfloat16)
    rows = left.shape[0]
    col_slots = out.shape[1] // PW
    row_local = lax.broadcasted_iota(jnp.int32, (rows, PW), 0)
    slot = g * ROW_GROUP + row_local // BS
    global_row = (slot * wide_count + wide_index) * BS + row_local % BS
    col_in_block = lax.broadcasted_iota(jnp.int32, (rows, PW), 1)
    dims = (((1,), (1,)), ((), ()))
    for t in range(col_slots):
        cols = pl.ds(t * PW, PW)
        column_block = t * narrow_count + narrow_index
        high = rhs_high[cols, :]
        low = rhs_low[cols, :]
        product = lax.dot_general(left_high, high, dims, preferred_element_type=jnp.float32)
        product += lax.dot_general(left_high, low, dims, preferred_element_type=jnp.float32)
        product += lax.dot_general(left_low, high, dims, preferred_element_type=jnp.float32)
        below = global_row >= column_block * PW + col_in_block
        take = mask[:, cols] > 0
        for part, kept in enumerate((kept0, kept1, kept2, kept3)):
            rows_here = slice(part * BS, (part + 1) * BS)
            there = take & (present[g * ROW_GROUP + part] > 0)
            base = front[rows_here, cols] + jnp.where(there, kept[:, cols], 0.0)
            value = base - product[rows_here]
            if t == 0:
                value = jnp.where(column_block > 0, value, left[rows_here])
            out[rows_here, cols] = jnp.where(below[rows_here], value, 0.0)


def update(front, child, kept_row, present, where, mask, factor, rhs):
    local_rows, local_cols = front.shape
    tall = ROW_GROUP * BS

    def kept_spec(part):
        return pl.BlockSpec(
            (BS, local_cols), lambda g, kept_row, present, where: (kept_row[g * ROW_GROUP + part], 0)
        )

    def fixed(shape):
        return pl.BlockSpec(shape, lambda g, kept_row, present, where: (0, 0))

    def tall_spec(width):
        return pl.BlockSpec((tall, width), lambda g, kept_row, present, where: (g, 0))

    return pl.pallas_call(
        update_kernel,
        out_shape=jax.ShapeDtypeStruct(front.shape, jnp.float32),
        grid_spec=pltpu.PrefetchScalarGridSpec(
            num_scalar_prefetch=3,
            grid=(local_rows // tall,),
            in_specs=[tall_spec(local_cols)]
            + [kept_spec(part) for part in range(ROW_GROUP)]
            + [
                fixed((1, local_cols)),
                tall_spec(PW),
                fixed((local_cols, PW)),
            ],
            out_specs=tall_spec(local_cols),
            scratch_shapes=[
                pltpu.VMEM((local_cols, PW), jnp.bfloat16),
                pltpu.VMEM((local_cols, PW), jnp.bfloat16),
            ],
        ),
        compiler_params=pltpu.CompilerParams(vmem_limit_bytes=VMEM_BYTES),
        cost_estimate=SMALL_COST,
        name="trailing_update",
    )(kept_row, present, where, front, child, child, child, child, mask, factor, rhs)


def shards(front, child_update, child_map):
    wide_count = lax.axis_size("wide")
    narrow_count = lax.axis_size("narrow")
    wide_index = lax.axis_index("wide")
    narrow_index = lax.axis_index("narrow")
    half_count = wide_count // 2
    local_rows, local_cols = front.shape
    front_slots = local_rows // BS
    col_slots = local_cols // PW
    col_tiles = local_cols // BS
    block_total = front_slots * wide_count
    child_side = wide_index // half_count
    partner = wide_index ^ half_count
    core = narrow_index % 2
    total = 2 * front_slots * col_tiles
    first_split = min(FIRST, total // 2)

    _, send_need = tile_tables(child_map, wide_index, front_slots, col_tiles)
    got_rows, got_need = tile_tables(child_map, partner, front_slots, col_tiles)
    send_counts = jnp.sum(send_need, axis=1).astype(jnp.int32)
    got_counts = jnp.sum(got_need, axis=1).astype(jnp.int32)
    own_need = jnp.where(core == 0, send_need[0], send_need[1])
    got_list = sending_list(jnp.where(core == 0, got_need[0], got_need[1]))
    send_second = jnp.maximum(send_counts[0], first_split)
    send_base = jnp.where(core == 0, 0, send_second)
    send_place = jnp.where(own_need, send_base + ranks(own_need), -1).astype(jnp.int32)
    got_base = jnp.where(core == 0, 0, jnp.maximum(got_counts[0], first_split))
    got_count = jnp.where(core == 0, got_counts[0], got_counts[1])
    pack_info = jnp.stack([(1 - child_side) * front_slots, core]).astype(jnp.int32)

    head_split = min(HEAD, total)
    has_more = total > HEAD

    def joined(kept_half, swapped, low):
        at = low + jnp.arange(kept_half.shape[0], dtype=jnp.int32)
        is_own = (at >= send_second) == (core == 1)
        return jnp.where(is_own[:, None, None], kept_half, swapped)

    own_map = lax.dynamic_slice_in_dim(child_map, (wide_index * 2 + child_side) * front_slots, front_slots)
    target = wide_index + wide_count * jnp.arange(front_slots, dtype=jnp.int32)
    kept_hit = own_map[None, :] == target[:, None]
    present = jnp.any(kept_hit, axis=1).astype(jnp.int32)
    kept_slot = jnp.sum(jnp.where(kept_hit, jnp.arange(front_slots, dtype=jnp.int32)[None, :], 0), axis=1)
    kept_row = (child_side * front_slots + kept_slot).astype(jnp.int32)
    col_local = jnp.arange(local_cols, dtype=jnp.int32)
    global_col = (col_local // PW * narrow_count + narrow_index) * PW + col_local % PW
    names = lax.dynamic_slice_in_dim(child_map, child_side * block_total, block_total)
    named_cols = jnp.any(names[:, None] == (global_col // BS)[None, :], axis=0).astype(jnp.int32)[None, :]
    panel = panel_base(front, child_update, kept_row, present, named_cols[:, :PW])

    bounds = [0, first_split, head_split] + ([total] if has_more else [])
    packed = pack(child_update, pack_info, send_place, bounds, LATE if has_more else 0, front_slots)
    first = cross_first_core(packed[0], half_count)
    second = joined(packed[1], core_swap(packed[2]), first_split)
    if has_more:
        counts = lax.dynamic_index_in_dim(
            chip_counts(child_map, front_slots, col_tiles), narrow_index // 2, 1, keepdims=False
        )
        counts = jnp.maximum(counts, FIXED).reshape(wide_count // QUAD, QUAD)
        tops = lowest_top(counts, total)
        moved, giver_at, taker_at, _ = flows(counts, tops)
        send_top = tops[wide_index // QUAD]
        got_top = tops[partner // QUAD]
        member = wide_index % QUAD
        send_quad = (moved[wide_index // QUAD], giver_at[wide_index // QUAD], taker_at[wide_index // QUAD])
        got_quad = (moved[partner // QUAD], giver_at[partner // QUAD], taker_at[partner // QUAD])

        rest = joined(packed[3], core_swap(packed[4]), head_split)
        soon = rest[: SOON - head_split]

        given = [
            lax.dynamic_slice_in_dim(rest, send_quad[1][member, member ^ mask] - head_split, MOVES[mask - 1])
            for mask in range(1, QUAD)
        ]
        second, soon, given, rest, panel = lax.optimization_barrier((second, soon, given, rest, panel))
        taken = [cross(given[mask - 1], mask) for mask in range(1, QUAD)]
    second = cross(second, half_count)

    if has_more:
        got_soon = cross(soon, half_count)

    panel_count = jnp.where(
        narrow_index == 0, jnp.sum(got_need[0, : PIECES * front_slots]).astype(jnp.int32), 0
    )

    def add(matrix, tiles, first, last, low, high, other=None):
        begin = jnp.maximum(jnp.maximum(low - got_base, 0), first)
        end = jnp.minimum(jnp.minimum(high - got_base, got_count), last)
        info = jnp.stack(
            [
                begin,
                jnp.maximum(begin, end),
                got_base - low,
                core,
                jnp.int32(wide_count),
                narrow_index,
                jnp.int32(narrow_count),
            ]
        ).astype(jnp.int32)
        other = core_swap(tiles) if other is None else other
        return tile_add(matrix, tiles, other, info, got_list, got_rows, front_slots)

    if has_more:
        second, taken, first = lax.optimization_barrier((second, taken, first))
    heads = [
        (0, first_split, first[:first_split], first[first_split:]),
        (first_split, head_split, second, core_swap(second)),
    ]
    for low, high, tiles, other in heads:
        panel = add(panel, tiles, 0, panel_count, low, high, other)
    if has_more:
        following = rest[SOON - head_split : NEXT - head_split]
        panel, got_soon, following = lax.optimization_barrier((panel, got_soon, following))
        got_next = cross(following, half_count)
    panel = from_first(panel)

    window = local_cols * narrow_count
    window_slots = max(1, window // (BS * wide_count))
    pieces = far_pieces(panel[: window_slots * BS])
    if has_more:
        relayed = rest
        for mask in range(1, QUAD):
            at = send_quad[2][member ^ mask, member] - head_split
            kept_there = lax.dynamic_slice_in_dim(relayed, at, MOVES[mask - 1])
            valid = jnp.arange(MOVES[mask - 1], dtype=jnp.int32) < send_quad[0][member ^ mask, member]
            relayed = lax.dynamic_update_slice_in_dim(
                relayed, jnp.where(valid[:, None, None], taken[mask - 1], kept_there), at, 0
            )
        send_late = jnp.maximum(send_top - LATE, FIXED)
        got_late = jnp.maximum(got_top - LATE, FIXED)
        late = lax.dynamic_slice_in_dim(relayed, send_late - head_split, LATE)
        late, pieces, got_next = lax.optimization_barrier((late, pieces, got_next))
        got_late_tiles = cross(late, half_count)

    gathered = near_pieces(pieces)
    diag_half = gathered[0, 0].reshape(PW, PW // 2)
    by_rows = gathered.reshape(-1, PW // 2)[:window].reshape(col_slots, narrow_count, PW, PW // 2)

    def whole_rows(mine, others):
        return jnp.where(
            core == 0, jnp.concatenate([mine, others], 1), jnp.concatenate([others, mine], 1)
        )

    def rows_of(index):
        return lax.dynamic_index_in_dim(by_rows, index, 1, keepdims=False).reshape(local_cols, PW // 2)

    diag_block = whole_rows(diag_half, core_swap(diag_half))
    if has_more:
        body = rest[NEXT - head_split : FIXED - head_split]
        diag_block, body = lax.optimization_barrier((diag_block, body))
        got_body = cross(body, half_count)
    raw_rows = whole_rows(rows_of(narrow_index), core_swap(rows_of(narrow_index ^ 1)))
    factor_diag, inverse = factor_block(diag_block)
    if has_more:
        inverse, got_late_tiles = lax.optimization_barrier((inverse, got_late_tiles))
        padded = jnp.concatenate([got_late_tiles, jnp.zeros_like(got_late_tiles[: max(MOVES)])], 0)
        given_back = [
            lax.dynamic_slice_in_dim(padded, got_quad[2][member ^ mask, member] - got_late, MOVES[mask - 1])
            for mask in range(1, QUAD)
        ]
        inverse, given_back = lax.optimization_barrier((inverse, given_back))
        returned = [cross(given_back[mask - 1], mask) for mask in range(1, QUAD)]

    where = jnp.stack(
        [wide_index, jnp.int32(wide_count), narrow_index, jnp.int32(narrow_count)]
    ).astype(jnp.int32)
    factor = solve(panel, inverse, factor_diag, where, True)
    panel_rows = solve(raw_rows, inverse, factor_diag, where, False)
    matrix = update(front, child_update, kept_row, present, where, named_cols, factor, panel_rows)

    for low, high, tiles, other in heads:
        matrix = add(matrix, tiles, panel_count, total, low, high, other)
    if has_more:
        matrix = add(matrix, got_soon, panel_count, total, head_split, SOON)
        matrix = add(matrix, got_late_tiles, panel_count, total, got_late, got_top)
        matrix = add(matrix, got_next, panel_count, total, SOON, NEXT)
        matrix, got_body, returned = lax.optimization_barrier((matrix, got_body, returned))
        steps = jnp.maximum((jnp.max(tops) - LATE - FIXED + CHUNK - 1) // CHUNK, 1)

        def add_held(matrix):
            matrix = add(matrix, got_body, panel_count, total, NEXT, FIXED)
            for mask in range(1, QUAD):
                low = got_quad[1][member, member ^ mask]
                high = low + got_quad[0][member, member ^ mask]
                matrix = add(matrix, returned[mask - 1], panel_count, total, low, high)
            return matrix

        def add_chunk(matrix, tiles, i):
            low = FIXED + (i - 1) * CHUNK
            return add(matrix, tiles, panel_count, total, low, jnp.minimum(low + CHUNK, got_late))

        def tail(i, carried):
            matrix, tiles = carried
            low = FIXED + i * CHUNK
            got = cross(lax.dynamic_slice_in_dim(relayed, low - head_split, CHUNK), half_count)
            matrix = lax.cond(i == 0, add_held, lambda matrix: add_chunk(matrix, tiles, i), matrix)
            return matrix, got

        matrix, last = lax.fori_loop(0, steps, tail, (matrix, got_body[:CHUNK]))
        matrix = add_chunk(matrix, last, steps)
    return matrix


def solution(mesh):
    placed = (P("wide", "narrow"), P("wide", "narrow"), P())
    return jax.shard_map(
        shards, mesh=mesh, in_specs=placed, out_specs=P("wide", "narrow"), check_vma=False
    )
```

```python
import functools

import jax
import jax.numpy as jnp
import numpy as np
from jax import lax
from jax.experimental import pallas as pl
from jax.experimental.pallas import tpu as pltpu
from jax.sharding import PartitionSpec as P

BS = 128
PW = 512
HALF = BS // 2
PIECES = PW // BS
FIRST = 40
HEAD = 88
SOON = 112
NEXT = 136
FIXED = 200
LATE = 96
MOVES = (64, 64, 40)
CHUNK = 16
QUAD = 4
STRIP = 8
STRIPS = 4
RING = 8
ROW_GROUP = 4
VMEM_BYTES = 56 * 1024 * 1024
SMALL_COST = pl.CostEstimate(flops=1024, bytes_accessed=1024, transcendentals=0)

HIGHEST_PRECISION = lax.Precision.HIGHEST


def cross(value, half_count):
    size = lax.axis_size("wide")
    return lax.ppermute(value, "wide", [(i, i ^ half_count) for i in range(size)])


def cross_first_core(value, half_count):
    narrow = lax.axis_size("narrow")
    size = lax.axis_size("wide") * narrow
    pairs = [(i, i ^ half_count * narrow) for i in range(0, size, 2)]
    return lax.ppermute(value, ("wide", "narrow"), pairs)


def core_swap(value):
    size = lax.axis_size("narrow")
    return lax.ppermute(value, "narrow", [(i, i ^ 1) for i in range(size)])


def from_first(value):
    size = lax.axis_size("narrow")
    if size == 2:
        moved = lax.ppermute(value, "narrow", [(0, 1)])
        return jnp.where(lax.axis_index("narrow") == 0, value, moved)
    mine = jnp.where(lax.axis_index("narrow") == 0, value, jnp.zeros_like(value))
    return lax.psum(mine, "narrow")


def far_pieces(piece):
    wide_count = lax.axis_size("wide")
    half_cols = piece.shape[1] // 2
    mine = lax.dynamic_slice_in_dim(piece, lax.axis_index("narrow") % 2 * half_cols, half_cols, 1)
    return [mine] + [cross(mine, mask) for mask in range(QUAD, wide_count, QUAD)]


def near_pieces(pieces):
    wide_index = lax.axis_index("wide")
    far = jnp.stack(pieces)
    quads, rows, half_cols = far.shape
    each = jnp.stack([far] + [cross(far, mask) for mask in range(1, QUAD)])
    bits = (QUAD * quads).bit_length() - 1
    each = each.reshape((2,) * bits + (rows, half_cols))
    masks = [QUAD >> shift for shift in range(1, QUAD.bit_length())]
    masks += [(QUAD * quads) >> shift for shift in range(1, quads.bit_length())]
    for axis, mask in enumerate(masks):
        each = jnp.where(wide_index // mask % 2 == 1, jnp.flip(each, axis), each)
    each = each.reshape(QUAD, quads, rows // BS, BS, half_cols)
    return each.transpose(2, 1, 0, 3, 4)


def tile_tables(child_map, source, front_slots, col_tiles):
    wide_count = lax.axis_size("wide")
    narrow_count = lax.axis_size("narrow")
    block_total = front_slots * wide_count
    side = source // (wide_count // 2)
    rows = lax.dynamic_slice_in_dim(child_map, (source * 2 + 1 - side) * front_slots, front_slots)
    names = lax.dynamic_slice_in_dim(child_map, side * block_total, block_total)
    tiles = jnp.arange(col_tiles, dtype=jnp.int32)
    first_core = lax.axis_index("narrow") // 2 * 2
    cores = first_core + jnp.arange(2, dtype=jnp.int32)
    global_tile = (tiles[None] // PIECES * narrow_count + cores[:, None]) * PIECES + tiles[None] % PIECES
    named = jnp.any(names[None, None, :] == global_tile[:, :, None], axis=2)
    need = named[:, :, None] & (rows[None, None, :] >= global_tile[:, :, None])
    need = need.reshape(2, col_tiles * front_slots)
    return rows, need


def chip_counts(child_map, front_slots, col_tiles):
    wide_count = lax.axis_size("wide")
    narrow_count = lax.axis_size("narrow")
    sides = jnp.arange(wide_count, dtype=jnp.int32) // (wide_count // 2)
    rows = child_map.reshape(wide_count, 2, front_slots)
    rows = jnp.where((sides == 0)[:, None], rows[:, 1], rows[:, 0])
    names = child_map.reshape(2, front_slots * wide_count)
    tiles = jnp.arange(col_tiles * narrow_count, dtype=jnp.int32)
    named = jnp.any(names[:, None, :] == tiles[None, :, None], axis=2)
    named = jnp.where((sides == 0)[:, None], named[:1], named[1:])
    each = jnp.sum(named[:, None, :] & (rows[:, :, None] >= tiles[None, None, :]), axis=1).astype(jnp.int32)
    each = each.reshape(wide_count, col_tiles // PIECES, narrow_count // 2, 2, PIECES)
    each = jnp.sum(each, axis=(1, 4))
    return jnp.maximum(each[..., 0], min(FIRST, front_slots * col_tiles)) + each[..., 1]


def ranks(need):
    order = jnp.arange(need.shape[0], dtype=jnp.int32)
    return jnp.sum((order[None, :] < order[:, None]) & need[None, :], axis=1).astype(jnp.int32)


def sending_list(need):
    order = jnp.arange(need.shape[0], dtype=jnp.int32)
    hit = (ranks(need)[None, :] == order[:, None]) & need[None, :]
    return jnp.sum(jnp.where(hit, order[None, :], 0), axis=1).astype(jnp.int32)


def flows(counts, top):
    give = jnp.maximum(counts - top[..., None], 0)
    take = jnp.clip(top[..., None] - counts, 0, LATE)
    give_from = jnp.cumsum(give, axis=-1) - give
    take_from = jnp.cumsum(take, axis=-1) - take
    begin = jnp.maximum(give_from[..., :, None], take_from[..., None, :])
    end = jnp.minimum((give_from + give)[..., :, None], (take_from + take)[..., None, :])
    moved = jnp.maximum(end - begin, 0)
    chips = np.arange(QUAD)
    limits = np.array((0,) + MOVES)[chips[:, None] ^ chips[None, :]]
    feasible = (jnp.sum(give, axis=-1) <= jnp.sum(take, axis=-1)) & jnp.all(moved <= limits, axis=(-2, -1))
    giver_at = top[..., None, None] + begin - give_from[..., :, None]
    taker_at = (top[..., None] - take - take_from)[..., None, :] + begin
    return moved, giver_at, taker_at, feasible


def lowest_top(counts, total):
    tops = FIXED + 4 * jnp.arange((total - FIXED) // 4 + 1, dtype=jnp.int32)
    _, _, _, feasible = flows(counts[None], jnp.broadcast_to(tops[:, None], (tops.shape[0], counts.shape[0])))
    return jnp.min(jnp.where(feasible, tops[:, None], total), axis=0).astype(jnp.int32)


def pack_kernel(bounds, front_slots, info, place, child, *refs):
    group, half = info[0], info[1]
    col_tiles = place.shape[0] // front_slots
    strips, in_sem, out_sem = refs[-3:]
    targets = [(0, bounds[1], refs[0], refs[0], bounds[1])]
    for part, (low, high) in enumerate(zip(bounds[1:], bounds[2:])):
        targets.append((low, high, refs[2 * part + 1], refs[2 * part + 2], 0))

    def strip_in(j):
        slot = j % STRIPS
        row = pl.multiple_of((group + j) * BS, BS)
        return pltpu.make_async_copy(child.at[pl.ds(row, BS)], strips.at[slot], in_sem.at[slot])

    def tile_out(j, c, spot, kept_half, sent_half, later):
        slot = j % STRIPS
        col = pl.multiple_of(c * BS, BS)
        own = pl.multiple_of(half * HALF, HALF)
        other = pl.multiple_of((1 - half) * HALF, HALF)
        return (
            pltpu.make_async_copy(
                strips.at[slot, pl.ds(own, HALF), pl.ds(col, BS)], kept_half.at[spot], out_sem.at[0, slot]
            ),
            pltpu.make_async_copy(
                strips.at[slot, pl.ds(other, HALF), pl.ds(col, BS)], sent_half.at[later + spot], out_sem.at[1, slot]
            ),
        )

    def each_tile(j, act):
        def one(c, carry):
            spot = place[c * front_slots + j]

            for low, high, kept_half, sent_half, later in targets:

                @pl.when((spot >= low) & (spot < high))
                def _():
                    for copy in tile_out(j, c, spot - low, kept_half, sent_half, later):
                        act(copy)

            return carry

        lax.fori_loop(0, col_tiles, one, 0)

    for j in range(min(STRIPS - 1, front_slots)):
        strip_in(j).start()
    for j in range(front_slots):
        strip_in(j).wait()
        each_tile(j, lambda copy: copy.start())
        if j >= 1:
            each_tile(j - 1, lambda copy: copy.wait())
        if j + STRIPS - 1 < front_slots:
            strip_in(j + STRIPS - 1).start()
    each_tile(front_slots - 1, lambda copy: copy.wait())


def pack(child, info, place, bounds, room, front_slots):
    sizes = [high - low for low, high in zip(bounds[1:], bounds[2:])]
    sizes[-1] += room
    sizes = [2 * bounds[1]] + [size for size in sizes for _ in range(2)]
    shapes = tuple(jax.ShapeDtypeStruct((size, HALF, BS), jnp.float32) for size in sizes)
    smem = pl.BlockSpec(memory_space=pltpu.SMEM)
    hbm = pl.BlockSpec(memory_space=pl.ANY)
    return pl.pallas_call(
        functools.partial(pack_kernel, tuple(bounds), front_slots),
        out_shape=shapes,
        in_specs=[smem, smem, hbm],
        out_specs=(hbm,) * len(shapes),
        scratch_shapes=[
            pltpu.VMEM((STRIPS, BS, child.shape[1]), jnp.float32),
            pltpu.SemaphoreType.DMA((STRIPS,)),
            pltpu.SemaphoreType.DMA((2, STRIPS)),
        ],
        compiler_params=pltpu.CompilerParams(vmem_limit_bytes=VMEM_BYTES),
        cost_estimate=SMALL_COST,
        name="pack_tiles",
    )(info, place, child)


def tile_add_kernel(front_slots, info, listed, rows, acc_in, own, other, acc, held, part, done, in_sem, out_sem):
    begin, end, place, half = info[0], info[1], info[2], info[3]
    wide_count, narrow_index, narrow_count = info[4], info[5], info[6]

    def spot(i):
        k = listed[i]
        col_tile = k // front_slots
        row_block = rows[k % front_slots]
        row = pl.multiple_of(row_block // wide_count * BS, BS)
        col = pl.multiple_of(col_tile * BS, BS)
        global_tile = (col_tile // PIECES * narrow_count + narrow_index) * PIECES + col_tile % PIECES
        return row, col, row_block == global_tile

    def copies_in(i):
        slot = i % RING
        row, col, _ = spot(i)
        at = place + i
        mine = pl.multiple_of(half * HALF, HALF)
        its = pl.multiple_of((1 - half) * HALF, HALF)
        return (
            pltpu.make_async_copy(acc.at[pl.ds(row, BS), pl.ds(col, BS)], held.at[slot], in_sem.at[0, slot]),
            pltpu.make_async_copy(own.at[at], part.at[slot, pl.ds(mine, HALF)], in_sem.at[1, slot]),
            pltpu.make_async_copy(other.at[at], part.at[slot, pl.ds(its, HALF)], in_sem.at[2, slot]),
        )

    def copy_out(i):
        slot = i % RING
        row, col, _ = spot(i)
        return pltpu.make_async_copy(done.at[slot], acc.at[pl.ds(row, BS), pl.ds(col, BS)], out_sem.at[slot])

    def issue(i):
        @pl.when(i < end)
        def _():
            for copy in copies_in(i):
                copy.start()

    for ahead in range(RING - 1):
        issue(begin + ahead)

    def step(i, carry):
        issue(i + RING - 1)
        for copy in copies_in(i):
            copy.wait()

        @pl.when(i - RING >= begin)
        def _():
            copy_out(i - RING).wait()

        slot = i % RING
        _, _, diagonal = spot(i)
        below = lax.broadcasted_iota(jnp.int32, (BS, BS), 0) >= lax.broadcasted_iota(jnp.int32, (BS, BS), 1)
        total = held[slot] + part[slot]
        done[slot] = jnp.where(below | jnp.logical_not(diagonal), total, 0.0)
        copy_out(i).start()
        return carry

    lax.fori_loop(begin, end, step, 0)

    def drain(i, carry):
        copy_out(i).wait()
        return carry

    lax.fori_loop(jnp.maximum(begin, end - RING), end, drain, 0)


def tile_add(acc, own, other, info, listed, rows, front_slots):
    smem = pl.BlockSpec(memory_space=pltpu.SMEM)
    hbm = pl.BlockSpec(memory_space=pl.ANY)
    return pl.pallas_call(
        functools.partial(tile_add_kernel, front_slots),
        out_shape=jax.ShapeDtypeStruct(acc.shape, acc.dtype),
        in_specs=[smem, smem, smem, hbm, hbm, hbm],
        out_specs=hbm,
        scratch_shapes=[
            pltpu.VMEM((RING, BS, BS), jnp.float32),
            pltpu.VMEM((RING, BS, BS), jnp.float32),
            pltpu.VMEM((RING, BS, BS), jnp.float32),
            pltpu.SemaphoreType.DMA((3, RING)),
            pltpu.SemaphoreType.DMA((RING,)),
        ],
        input_output_aliases={3: 0},
        cost_estimate=SMALL_COST,
        name="add_tiles",
    )(info, listed, rows, acc, own, other)


def panel_base_kernel(kept_row, present, front, kept, mask, out):
    s = pl.program_id(0)
    take = (mask[...] > 0) & (present[s] > 0)
    out[...] = front[...] + jnp.where(take, kept[...], 0.0)


def panel_base(front, child, kept_row, present, mask):
    local_rows = front.shape[0]
    return pl.pallas_call(
        panel_base_kernel,
        out_shape=jax.ShapeDtypeStruct((local_rows, PW), jnp.float32),
        grid_spec=pltpu.PrefetchScalarGridSpec(
            num_scalar_prefetch=2,
            grid=(local_rows // BS,),
            in_specs=[
                pl.BlockSpec((BS, PW), lambda s, kept_row, present: (s, 0)),
                pl.BlockSpec((BS, PW), lambda s, kept_row, present: (kept_row[s], 0)),
                pl.BlockSpec((1, PW), lambda s, kept_row, present: (0, 0)),
            ],
            out_specs=pl.BlockSpec((BS, PW), lambda s, kept_row, present: (s, 0)),
        ),
        cost_estimate=SMALL_COST,
        name="panel_base",
    )(kept_row, present, front, child, mask)


def exact_dot(left, right, contract):
    return lax.dot_general(
        left, right, (contract, ((), ())), precision=HIGHEST_PRECISION, preferred_element_type=jnp.float32
    )


def factor_kernel(diag, lower, inverse, work, pair):
    size = diag.shape[0]
    full = diag[...]
    row = lax.broadcasted_iota(jnp.int32, (size, size), 0)
    col = lax.broadcasted_iota(jnp.int32, (size, size), 1)
    work[...] = jnp.where(row >= col, full, full.T)
    lower[...] = jnp.zeros_like(lower)
    inverse[...] = jnp.zeros_like(inverse)
    block_row = lax.broadcasted_iota(jnp.int32, (BS, BS), 0)
    block_col = lax.broadcasted_iota(jnp.int32, (BS, BS), 1)
    strip_row = lax.broadcasted_iota(jnp.int32, (STRIP, 2 * BS), 0)
    strip_lane = lax.broadcasted_iota(jnp.int32, (STRIP, 2 * BS), 1)
    for k in range(size // BS):
        here = slice(k * BS, (k + 1) * BS)
        pair[:, :BS] = work[here, here]
        pair[:, BS:] = jnp.where(block_row == block_col, 1.0, 0.0)

        def eliminate(step, carry):
            top = pl.multiple_of(step * STRIP, STRIP)
            strip = pair[pl.ds(top, STRIP), :]
            for j in range(STRIP):
                column = jnp.sum(jnp.where(strip_lane == top + j, strip, 0.0), axis=1, keepdims=True)
                scale = lax.rsqrt(column[j : j + 1])
                pivot = strip[j : j + 1] * scale
                reduced = strip - (column * scale) * pivot
                strip = jnp.where(strip_row > j, reduced, jnp.where(strip_row == j, pivot, strip))
            pair[pl.ds(top, STRIP), :] = strip
            ahead = jnp.where(strip_lane[:, :BS] >= top + STRIP, strip[:, :BS], 0.0)
            pair[...] -= exact_dot(ahead.T, strip, ((1,), (0,)))
            return carry

        lax.fori_loop(0, BS // STRIP, eliminate, 0)
        own_inverse = jnp.where(block_row >= block_col, pair[:, BS:], 0.0)
        lower[here, here] = jnp.where(block_row <= block_col, pair[:, :BS], 0.0).T
        inverse[here, here] = own_inverse
        if (k + 1) * BS < size:
            below = slice((k + 1) * BS, size)
            column_block = exact_dot(work[below, here], own_inverse, ((1,), (1,)))
            lower[below, here] = column_block
            work[below, below] -= exact_dot(column_block, column_block, ((1,), (1,)))
        if k:
            before = slice(0, k * BS)
            product = exact_dot(lower[here, before], inverse[before, before], ((1,), (0,)))
            inverse[here, before] = -exact_dot(own_inverse, product, ((1,), (0,)))


def factor_block(diag):
    shape = jax.ShapeDtypeStruct(diag.shape, jnp.float32)
    return pl.pallas_call(
        factor_kernel,
        out_shape=(shape, shape),
        scratch_shapes=[pltpu.VMEM(diag.shape, jnp.float32), pltpu.VMEM((BS, 2 * BS), jnp.float32)],
        compiler_params=pltpu.CompilerParams(vmem_limit_bytes=VMEM_BYTES),
        cost_estimate=SMALL_COST,
        name="factor_block",
    )(diag)


def solve_kernel(with_diagonal, where, rows, inverse, lower, out):
    out[...] = exact_dot(rows[...], inverse[...], ((1,), (1,)))
    if with_diagonal:
        wide_index, wide_count = where[0], where[1]
        for part in range(rows.shape[0] // BS):
            row_block = (pl.program_id(0) * ROW_GROUP + part) * wide_count + wide_index

            @pl.when(row_block < PIECES)
            def _():
                start = pl.multiple_of(row_block * BS, BS)
                out[part * BS : (part + 1) * BS, :] = lower[pl.ds(start, BS), :]


def solve(rows, inverse, lower, where, with_diagonal):
    tall = ROW_GROUP * BS
    whole = pl.BlockSpec((PW, PW), lambda g, where: (0, 0))
    strip = pl.BlockSpec((tall, PW), lambda g, where: (g, 0))
    return pl.pallas_call(
        functools.partial(solve_kernel, with_diagonal),
        out_shape=jax.ShapeDtypeStruct(rows.shape, jnp.float32),
        grid_spec=pltpu.PrefetchScalarGridSpec(
            num_scalar_prefetch=1,
            grid=(rows.shape[0] // tall,),
            in_specs=[strip, whole, whole],
            out_specs=strip,
        ),
        compiler_params=pltpu.CompilerParams(vmem_limit_bytes=VMEM_BYTES),
        cost_estimate=SMALL_COST,
        name="solve_rows",
    )(where, rows, inverse, lower)


def update_kernel(kept_row, present, where, front, kept0, kept1, kept2, kept3, mask, factor, rhs, out, rhs_high, rhs_low):
    g = pl.program_id(0)

    @pl.when(g == 0)
    def _():
        rhs_high[...] = rhs[...].astype(jnp.bfloat16)
        rhs_low[...] = (rhs[...] - rhs_high[...].astype(jnp.float32)).astype(jnp.bfloat16)

    wide_index, wide_count, narrow_index, narrow_count = where[0], where[1], where[2], where[3]
    left = factor[...]
    left_high = left.astype(jnp.bfloat16)
    left_low = (left - left_high.astype(jnp.float32)).astype(jnp.bfloat16)
    rows = left.shape[0]
    col_slots = out.shape[1] // PW
    row_local = lax.broadcasted_iota(jnp.int32, (rows, PW), 0)
    slot = g * ROW_GROUP + row_local // BS
    global_row = (slot * wide_count + wide_index) * BS + row_local % BS
    col_in_block = lax.broadcasted_iota(jnp.int32, (rows, PW), 1)
    dims = (((1,), (1,)), ((), ()))
    for t in range(col_slots):
        cols = pl.ds(t * PW, PW)
        column_block = t * narrow_count + narrow_index
        high = rhs_high[cols, :]
        low = rhs_low[cols, :]
        product = lax.dot_general(left_high, high, dims, preferred_element_type=jnp.float32)
        product += lax.dot_general(left_high, low, dims, preferred_element_type=jnp.float32)
        product += lax.dot_general(left_low, high, dims, preferred_element_type=jnp.float32)
        below = global_row >= column_block * PW + col_in_block
        take = mask[:, cols] > 0
        for part, kept in enumerate((kept0, kept1, kept2, kept3)):
            rows_here = slice(part * BS, (part + 1) * BS)
            there = take & (present[g * ROW_GROUP + part] > 0)
            base = front[rows_here, cols] + jnp.where(there, kept[:, cols], 0.0)
            value = base - product[rows_here]
            if t == 0:
                value = jnp.where(column_block > 0, value, left[rows_here])
            out[rows_here, cols] = jnp.where(below[rows_here], value, 0.0)


def update(front, child, kept_row, present, where, mask, factor, rhs):
    local_rows, local_cols = front.shape
    tall = ROW_GROUP * BS

    def kept_spec(part):
        return pl.BlockSpec(
            (BS, local_cols), lambda g, kept_row, present, where: (kept_row[g * ROW_GROUP + part], 0)
        )

    def fixed(shape):
        return pl.BlockSpec(shape, lambda g, kept_row, present, where: (0, 0))

    def tall_spec(width):
        return pl.BlockSpec((tall, width), lambda g, kept_row, present, where: (g, 0))

    return pl.pallas_call(
        update_kernel,
        out_shape=jax.ShapeDtypeStruct(front.shape, jnp.float32),
        grid_spec=pltpu.PrefetchScalarGridSpec(
            num_scalar_prefetch=3,
            grid=(local_rows // tall,),
            in_specs=[tall_spec(local_cols)]
            + [kept_spec(part) for part in range(ROW_GROUP)]
            + [
                fixed((1, local_cols)),
                tall_spec(PW),
                fixed((local_cols, PW)),
            ],
            out_specs=tall_spec(local_cols),
            scratch_shapes=[
                pltpu.VMEM((local_cols, PW), jnp.bfloat16),
                pltpu.VMEM((local_cols, PW), jnp.bfloat16),
            ],
        ),
        compiler_params=pltpu.CompilerParams(vmem_limit_bytes=VMEM_BYTES),
        cost_estimate=SMALL_COST,
        name="trailing_update",
    )(kept_row, present, where, front, child, child, child, child, mask, factor, rhs)


def shards(front, child_update, child_map):
    wide_count = lax.axis_size("wide")
    narrow_count = lax.axis_size("narrow")
    wide_index = lax.axis_index("wide")
    narrow_index = lax.axis_index("narrow")
    half_count = wide_count // 2
    local_rows, local_cols = front.shape
    front_slots = local_rows // BS
    col_slots = local_cols // PW
    col_tiles = local_cols // BS
    block_total = front_slots * wide_count
    child_side = wide_index // half_count
    partner = wide_index ^ half_count
    core = narrow_index % 2
    total = 2 * front_slots * col_tiles
    first_split = min(FIRST, total // 2)

    _, send_need = tile_tables(child_map, wide_index, front_slots, col_tiles)
    got_rows, got_need = tile_tables(child_map, partner, front_slots, col_tiles)
    send_counts = jnp.sum(send_need, axis=1).astype(jnp.int32)
    got_counts = jnp.sum(got_need, axis=1).astype(jnp.int32)
    own_need = jnp.where(core == 0, send_need[0], send_need[1])
    got_list = sending_list(jnp.where(core == 0, got_need[0], got_need[1]))
    send_second = jnp.maximum(send_counts[0], first_split)
    send_base = jnp.where(core == 0, 0, send_second)
    send_place = jnp.where(own_need, send_base + ranks(own_need), -1).astype(jnp.int32)
    got_base = jnp.where(core == 0, 0, jnp.maximum(got_counts[0], first_split))
    got_count = jnp.where(core == 0, got_counts[0], got_counts[1])
    pack_info = jnp.stack([(1 - child_side) * front_slots, core]).astype(jnp.int32)

    head_split = min(HEAD, total)
    has_more = total > HEAD

    def joined(kept_half, swapped, low):
        at = low + jnp.arange(kept_half.shape[0], dtype=jnp.int32)
        is_own = (at >= send_second) == (core == 1)
        return jnp.where(is_own[:, None, None], kept_half, swapped)

    own_map = lax.dynamic_slice_in_dim(child_map, (wide_index * 2 + child_side) * front_slots, front_slots)
    target = wide_index + wide_count * jnp.arange(front_slots, dtype=jnp.int32)
    kept_hit = own_map[None, :] == target[:, None]
    present = jnp.any(kept_hit, axis=1).astype(jnp.int32)
    kept_slot = jnp.sum(jnp.where(kept_hit, jnp.arange(front_slots, dtype=jnp.int32)[None, :], 0), axis=1)
    kept_row = (child_side * front_slots + kept_slot).astype(jnp.int32)
    col_local = jnp.arange(local_cols, dtype=jnp.int32)
    global_col = (col_local // PW * narrow_count + narrow_index) * PW + col_local % PW
    names = lax.dynamic_slice_in_dim(child_map, child_side * block_total, block_total)
    named_cols = jnp.any(names[:, None] == (global_col // BS)[None, :], axis=0).astype(jnp.int32)[None, :]
    panel = panel_base(front, child_update, kept_row, present, named_cols[:, :PW])

    bounds = [0, first_split, head_split] + ([total] if has_more else [])
    packed = pack(child_update, pack_info, send_place, bounds, LATE if has_more else 0, front_slots)
    first = cross_first_core(packed[0], half_count)
    second = joined(packed[1], core_swap(packed[2]), first_split)
    if has_more:
        counts = lax.dynamic_index_in_dim(
            chip_counts(child_map, front_slots, col_tiles), narrow_index // 2, 1, keepdims=False
        )
        counts = jnp.maximum(counts, FIXED).reshape(wide_count // QUAD, QUAD)
        tops = lowest_top(counts, total)
        moved, giver_at, taker_at, _ = flows(counts, tops)
        send_top = tops[wide_index // QUAD]
        got_top = tops[partner // QUAD]
        member = wide_index % QUAD
        send_quad = (moved[wide_index // QUAD], giver_at[wide_index // QUAD], taker_at[wide_index // QUAD])
        got_quad = (moved[partner // QUAD], giver_at[partner // QUAD], taker_at[partner // QUAD])

        rest = joined(packed[3], core_swap(packed[4]), head_split)
        soon = rest[: SOON - head_split]

        given = [
            lax.dynamic_slice_in_dim(rest, send_quad[1][member, member ^ mask] - head_split, MOVES[mask - 1])
            for mask in range(1, QUAD)
        ]
        second, soon, given, rest, panel = lax.optimization_barrier((second, soon, given, rest, panel))
        taken = [cross(given[mask - 1], mask) for mask in range(1, QUAD)]
    second = cross(second, half_count)

    if has_more:
        got_soon = cross(soon, half_count)

    panel_count = jnp.where(
        narrow_index == 0, jnp.sum(got_need[0, : PIECES * front_slots]).astype(jnp.int32), 0
    )

    def add(matrix, tiles, first, last, low, high, other=None):
        begin = jnp.maximum(jnp.maximum(low - got_base, 0), first)
        end = jnp.minimum(jnp.minimum(high - got_base, got_count), last)
        info = jnp.stack(
            [
                begin,
                jnp.maximum(begin, end),
                got_base - low,
                core,
                jnp.int32(wide_count),
                narrow_index,
                jnp.int32(narrow_count),
            ]
        ).astype(jnp.int32)
        other = core_swap(tiles) if other is None else other
        return tile_add(matrix, tiles, other, info, got_list, got_rows, front_slots)

    if has_more:
        second, taken, first = lax.optimization_barrier((second, taken, first))
    heads = [
        (0, first_split, first[:first_split], first[first_split:]),
        (first_split, head_split, second, core_swap(second)),
    ]
    for low, high, tiles, other in heads:
        panel = add(panel, tiles, 0, panel_count, low, high, other)
    if has_more:
        following = rest[SOON - head_split : NEXT - head_split]
        relayed = rest
        for mask in range(1, QUAD):
            at = send_quad[2][member ^ mask, member] - head_split
            kept_there = lax.dynamic_slice_in_dim(relayed, at, MOVES[mask - 1])
            valid = jnp.arange(MOVES[mask - 1], dtype=jnp.int32) < send_quad[0][member ^ mask, member]
            relayed = lax.dynamic_update_slice_in_dim(
                relayed, jnp.where(valid[:, None, None], taken[mask - 1], kept_there), at, 0
            )
        send_late = jnp.maximum(send_top - LATE, FIXED)
        got_late = jnp.maximum(got_top - LATE, FIXED)
        late = lax.dynamic_slice_in_dim(relayed, send_late - head_split, LATE)
        body = rest[NEXT - head_split : FIXED - head_split]
        panel, got_soon, following, late, body = lax.optimization_barrier(
            (panel, got_soon, following, late, body)
        )
        got_next = cross(following, half_count)
    panel = from_first(panel)

    window = local_cols * narrow_count
    window_slots = max(1, window // (BS * wide_count))
    pieces = far_pieces(panel[: window_slots * BS])
    if has_more:
        late, pieces, got_next = lax.optimization_barrier((late, pieces, got_next))
        got_late_tiles = cross(late, half_count)

    gathered = near_pieces(pieces)
    diag_half = gathered[0, 0].reshape(PW, PW // 2)
    by_rows = gathered.reshape(-1, PW // 2)[:window].reshape(col_slots, narrow_count, PW, PW // 2)

    def whole_rows(mine, others):
        return jnp.where(
            core == 0, jnp.concatenate([mine, others], 1), jnp.concatenate([others, mine], 1)
        )

    def rows_of(index):
        return lax.dynamic_index_in_dim(by_rows, index, 1, keepdims=False).reshape(local_cols, PW // 2)

    diag_block = whole_rows(diag_half, core_swap(diag_half))
    if has_more:
        diag_block, body = lax.optimization_barrier((diag_block, body))
        got_body = cross(body, half_count)
    raw_rows = whole_rows(rows_of(narrow_index), core_swap(rows_of(narrow_index ^ 1)))
    factor_diag, inverse = factor_block(diag_block)
    if has_more:
        inverse, got_late_tiles = lax.optimization_barrier((inverse, got_late_tiles))
        padded = jnp.concatenate([got_late_tiles, jnp.zeros_like(got_late_tiles[: max(MOVES)])], 0)
        given_back = [
            lax.dynamic_slice_in_dim(padded, got_quad[2][member ^ mask, member] - got_late, MOVES[mask - 1])
            for mask in range(1, QUAD)
        ]
        inverse, given_back = lax.optimization_barrier((inverse, given_back))
        returned = [cross(given_back[mask - 1], mask) for mask in range(1, QUAD)]

    where = jnp.stack(
        [wide_index, jnp.int32(wide_count), narrow_index, jnp.int32(narrow_count)]
    ).astype(jnp.int32)
    factor = solve(panel, inverse, factor_diag, where, True)
    panel_rows = solve(raw_rows, inverse, factor_diag, where, False)
    matrix = update(front, child_update, kept_row, present, where, named_cols, factor, panel_rows)

    for low, high, tiles, other in heads:
        matrix = add(matrix, tiles, panel_count, total, low, high, other)
    if has_more:
        matrix = add(matrix, got_soon, panel_count, total, head_split, SOON)
        matrix = add(matrix, got_late_tiles, panel_count, total, got_late, got_top)
        matrix = add(matrix, got_next, panel_count, total, SOON, NEXT)
        matrix, got_body, returned = lax.optimization_barrier((matrix, got_body, returned))
        steps = jnp.maximum((jnp.max(tops) - LATE - FIXED + CHUNK - 1) // CHUNK, 1)

        def add_held(matrix):
            matrix = add(matrix, got_body, panel_count, total, NEXT, FIXED)
            for mask in range(1, QUAD):
                low = got_quad[1][member, member ^ mask]
                high = low + got_quad[0][member, member ^ mask]
                matrix = add(matrix, returned[mask - 1], panel_count, total, low, high)
            return matrix

        def add_chunk(matrix, tiles, i):
            low = FIXED + (i - 1) * CHUNK
            return add(matrix, tiles, panel_count, total, low, jnp.minimum(low + CHUNK, got_late))

        def tail(i, carried):
            matrix, tiles = carried
            low = FIXED + i * CHUNK
            got = cross(lax.dynamic_slice_in_dim(relayed, low - head_split, CHUNK), half_count)
            matrix = lax.cond(i == 0, add_held, lambda matrix: add_chunk(matrix, tiles, i), matrix)
            return matrix, got

        matrix, last = lax.fori_loop(0, steps, tail, (matrix, got_body[:CHUNK]))
        matrix = add_chunk(matrix, last, steps)
    return matrix


def solution(mesh):
    placed = (P("wide", "narrow"), P("wide", "narrow"), P())
    return jax.shard_map(
        shards, mesh=mesh, in_specs=placed, out_specs=P("wide", "narrow"), check_vma=False
    )
```
